256 devices in a mesh: pr: 8 (over z), pc: 8 (over x, core), gz: 4 (over y).
Axes of the slice: x: 4, y: 4, z: 8, core: 2. Of those that a mesh axis runs over, the one named last changes fastest.
Arguments:
- rhs_leaf: bfloat16 [4, 512, 128, 256], P('gz', ('pr', 'pc')), may hold values from -16 to 16
- rhs_mid: bfloat16 [4, 256, 256, 256], P('gz', ('pr', 'pc')), may hold values from -6 to 6
- rhs_top: bfloat16 [64, 512, 256], P('pr', 'pc'), may hold values from -6 to 6
- inv_leaf: bfloat16 [4, 512, 128, 128], P('gz', ('pr', 'pc')), may hold values from -1 to 1.5, as said below
- inv_mid: bfloat16 [4, 256, 256, 256], P('gz', ('pr', 'pc')), may hold values from -1 to 1.5, as said below
- inv_top: bfloat16 [64, 512, 512], P('pr', 'pc'), may hold values from -1 to 1.5, as said below
- off_leaf_mid: bfloat16 [4, 512, 256, 128], P('gz', ('pr', 'pc')), may hold values from -0.375 to 0.375
- off_leaf_top: bfloat16 [4, 512, 512, 128], P('gz', ('pr', 'pc')), may hold values from -0.25 to 0.25
- off_leaf_out: bfloat16 [4, 512, 1024, 128], P('gz', ('pr', 'pc')), may hold values from -0.0234375 to 0.0234375
- off_mid_top: bfloat16 [4, 256, 512, 256], P('gz', ('pr', 'pc')), may hold values from -0.1875 to 0.1875
- off_mid_out: bfloat16 [4, 256, 1024, 256], P('gz', ('pr', 'pc')), may hold values from -0.0234375 to 0.0234375
- off_top_out: bfloat16 [64, 1024, 512], P('pr', 'pc'), may hold values from -0.0625 to 0.0625
- parent_leaf: int32 [4, 512, 1], P('gz', ('pr', 'pc')), may hold values from 0 to 255, as said below
- parent_mid: int32 [4, 256, 1], P('gz', ('pr', 'pc')), may hold values from 0 to 63, as said below
- width_leaf: int32 [4, 512], P('gz', ('pr', 'pc')), may hold values from 1 to 128, 49152 in all within a row
- width_mid: int32 [4, 256], P('gz', ('pr', 'pc')), may hold values from 1 to 256, 49152 in all within a row
- width_top: int32 [64], P('pr'), may hold values from 1 to 512, 24576 in all
- pattern_leaf: int32 [4, 512, 2], P('gz', ('pr', 'pc')), may hold values 0 or 1
- pattern_mid: int32 [4, 256], P('gz', ('pr', 'pc')), may hold values 0 or 1
Outputs:
- leaf_solution: bfloat16 [4, 512, 128, 256], P('gz', ('pr', 'pc'))
- mid_solution: bfloat16 [4, 256, 256, 256], P('gz', ('pr', 'pc'))
- top_solution: bfloat16 [64, 512, 256], P(('pr', 'gz'), 'pc')
- outer_update: float32 [1024, 256], P('pc', ('pr', 'gz'))
The draws below stay inside these ranges and needn't reach their ends.
Inputs may be any that keep to these rules, and one draw needn't show every extreme that they name: `inv_leaf`: each 128 x 128 block is lower triangular with its diagonal between 0.5 and 1.5. `inv_mid`: each 256 x 256 block is lower triangular with its diagonal between 0.5 and 1.5. `inv_top`: each 512 x 512 block is lower triangular with its diagonal between 0.5 and 1.5. `parent_leaf`: the leaves in each aligned block of 8 (per layer) have their parents among the matching aligned block of 4 level-one supernodes, and each of those has exactly two of them as children. `parent_mid`: Level-one supernodes are taken in aligned blocks of 32 per layer, the i-th block lying under process row i; each one's parent is among the 8 level-two supernodes of that process row.
All inputs are finite; a program needn't handle non-finite values. No bound on the sum of `width_leaf` or of `width_mid` or of `width_top` or of `pattern_leaf` or of `pattern_mid` on one device may be relied on, other than what follows from the above.
Results may differ from the reference program's by a relative error of at most 0.0062.
Values may be sent and summed in bfloat16 or wider, within the bound.
A program may use at most 64 MiB of HBM per device.

```python
import math
import jax
import jax.numpy as jnp
import numpy as np

LEAF_DEV = 8
MID_DEV = 4
TOP_DEV = 8
LEAVES = 512
MIDS = 256
TOPS = 64
LEAF_W = 128
MID_W = 256
TOP_W = 512
OUTER_ROWS = 1024
RHS = 256
N_GZ = 4


def lower_inverse(key, lead_shape, width):
    key_strict, key_diag = jax.random.split(key)
    row_ids = jnp.arange(width)
    lower_mask = row_ids[:, None] > row_ids[None, :]
    diag_mask = row_ids[:, None] == row_ids[None, :]
    spread = 0.8 / math.sqrt(width)
    strict_part = jnp.clip(jax.random.normal(key_strict, lead_shape + (width, width), jnp.float32), -4.0, 4.0) * spread
    diag_part = jax.random.uniform(key_diag, lead_shape + (width, width), jnp.float32, 0.5, 1.5)
    blocks = jnp.where(lower_mask, strict_part, jnp.where(diag_mask, diag_part, 0.0))
    return blocks.astype(jnp.bfloat16)


def shuffled_positions(key, lead_shape, count):
    scores = jax.random.randint(key, lead_shape + (count,), 0, 1 << 16, dtype=jnp.int32)
    scores = scores * count + jnp.arange(count, dtype=jnp.int32)
    return jnp.argsort(scores, axis=-1, stable=True).astype(jnp.int32)


def draw_inv_leaf(key, part):
    key = jax.random.fold_in(key, 11)
    return lower_inverse(key, (N_GZ, LEAVES), LEAF_W)


def draw_inv_mid(key, part):
    key = jax.random.fold_in(key, 23)
    return lower_inverse(key, (N_GZ, MIDS), MID_W)


def draw_inv_top(key, part):
    key = jax.random.fold_in(key, 37)
    return lower_inverse(key, (TOPS,), TOP_W)


def draw_parent_leaf(key, part):
    key = jax.random.fold_in(key, 41)
    groups = LEAVES // LEAF_DEV
    order = shuffled_positions(key, (N_GZ, groups), LEAF_DEV)
    local = order % MID_DEV
    base = jnp.arange(groups, dtype=jnp.int32)[None, :, None] * MID_DEV
    return (base + local).reshape(N_GZ, LEAVES, 1).astype(jnp.int32)


def draw_parent_mid(key, part):
    key = jax.random.fold_in(key, 53)
    per_row = MIDS // (TOPS // TOP_DEV)
    rows = TOPS // TOP_DEV
    order = shuffled_positions(key, (N_GZ, rows), per_row)
    local = TOP_DEV - 1 - order % TOP_DEV
    base = jnp.arange(rows, dtype=jnp.int32)[None, :, None] * TOP_DEV
    return (base + local).reshape(N_GZ, MIDS, 1).astype(jnp.int32)


def touch_ends(entries, own_key, smallest, top_value):
    shape = entries.shape
    spot = [jax.random.randint(jax.random.fold_in(own_key, axis), (), 0, shape[axis]) for axis in range(len(shape))]
    entries = entries.at[tuple(spot)].set(smallest)
    longest = shape.index(max(shape))
    spot[longest] = (spot[longest] + 1) % shape[longest]
    return entries.at[tuple(spot)].set(top_value)


def strengthened(result, rng, source, target, parts, factor):
    def block_of(axis_at):
        return (jnp.arange(result.shape[axis_at]) // (result.shape[axis_at] // parts)).reshape((-1,) + (1,) * (result.ndim - 1 - axis_at))

    one_side = jax.random.permutation(rng, parts)[block_of(target)]
    far = (block_of(target) + parts // 2) % parts
    return jnp.where((block_of(source) == one_side) | (block_of(source) == far), factor * result, result)


def levels(key, dims, pieces, smallest, largest):
    def one(dim, parts):
        steps = jax.random.uniform(jax.random.fold_in(jax.random.fold_in(key, 6), dim), (parts,), jnp.float32, smallest / len(pieces), largest / len(pieces))
        return jnp.repeat(jnp.exp(steps), dims[dim] // parts).reshape((-1,) + (1,) * (len(dims) - dim - 1))

    level = one(*pieces[0])
    for cut in pieces[1:]:
        level = level * one(*cut)
    return level


def profile(amount, total, bound, lean):
    loads = [(1 << 20) // math.isqrt(grade ** lean) + 1 for grade in range(2, amount + 1)]
    surplus, given = total - bound - (amount - 1), [1] * (amount - 1)
    while surplus > 0:
        candidates = [i for i in range(amount - 1) if given[i] < bound]
        pool, budget = sum([loads[i] for i in candidates]), surplus
        for i in candidates:
            addition = min(bound - given[i], max(1, budget * loads[i] // pool), surplus)
            given[i] = given[i] + addition
            surplus = surplus - addition
    return np.array([bound] + given)


def ragged_sizes(own_key, number_of, total, reach, lean):
    if number_of == 2:
        one = jax.random.randint(own_key, (), max(1, total - reach), min(reach, total - 1) + 1)
        return jnp.stack([one, total - one])
    lengths = jnp.asarray(profile(number_of, total, reach, lean), jnp.int32)
    pairs = (number_of - 1) // 2
    giver, taker = lengths[1:1 + 2 * pairs:2], lengths[2:2 + 2 * pairs:2]
    margin = jnp.minimum(giver - 1, reach - taker)
    passed = jax.random.randint(jax.random.fold_in(own_key, 1), (pairs,), 0, 1 << 20) % (margin + 1)
    lengths = lengths.at[1:1 + 2 * pairs:2].set(giver - passed).at[2:2 + 2 * pairs:2].set(taker + passed)
    return lengths[jax.random.permutation(jax.random.fold_in(own_key, 2), number_of)]


def centred(key, dims, scale, bound, cuts=(), kind=jnp.bfloat16):
    gain = levels(key, dims, cuts, -0.22, 0.18) if cuts else 1.0
    drawn = jax.random.normal(key, dims, jnp.float32) * scale * gain
    return jnp.minimum(jnp.maximum(drawn, -bound), bound).astype(kind)


def gaussian_with(own_key, extent, scale, bound, cuts, heavy, kind=jnp.bfloat16):
    result = scale * jax.random.normal(own_key, extent, jnp.float32)
    if cuts:
        result = result * levels(own_key, extent, cuts, -0.22, 0.18)
    return jnp.clip(strengthened(result, jax.random.fold_in(own_key, 3), *heavy), -bound, bound).astype(kind)


def setup_inputs(seed: int = 0) -> dict:
    arg_keys = jax.random.split(jax.random.key(seed), 20)
    rhs_leaf = gaussian_with(arg_keys[0], (N_GZ, LEAVES, LEAF_W, RHS), 1.0, 16.0, ((0, 4), (1, 64)), (1, 3, 64, 4.0))
    rhs_mid = centred(arg_keys[1], (N_GZ, MIDS, MID_W, RHS), 1.0, 6.0, ((0, 4), (1, 64)))
    rhs_top = centred(arg_keys[2], (TOPS, TOP_W, RHS), 1.0, 6.0, ((0, 8), (1, 8)))
    inv_leaf = draw_inv_leaf(jax.random.fold_in(arg_keys[19], 71), 0)
    inv_mid = draw_inv_mid(jax.random.fold_in(arg_keys[19], 71), 0)
    inv_top = draw_inv_top(jax.random.fold_in(arg_keys[19], 71), 0)
    off_leaf_mid = centred(arg_keys[6], (N_GZ, LEAVES, MID_W, LEAF_W), (2 * LEAF_W) ** -0.5, 0.375, ((0, 4), (1, 64)))
    off_leaf_top = centred(arg_keys[7], (N_GZ, LEAVES, TOP_W, LEAF_W), (4 * LEAF_W) ** -0.5, 0.25, ((0, 4), (1, 64)))
    off_leaf_out = centred(arg_keys[8], (N_GZ, LEAVES, OUTER_ROWS, LEAF_W), (LEAF_W * N_GZ * LEAVES // 4) ** -0.5, 0.0234375, ((0, 4), (1, 64)))
    off_mid_top = centred(arg_keys[9], (N_GZ, MIDS, TOP_W, MID_W), (4 * MID_W) ** -0.5, 0.1875, ((0, 4), (1, 64)))
    off_mid_out = centred(arg_keys[10], (N_GZ, MIDS, OUTER_ROWS, MID_W), (MID_W * N_GZ * MIDS // 4) ** -0.5, 0.0234375, ((0, 4), (1, 64)))
    off_top_out = centred(arg_keys[11], (TOPS, OUTER_ROWS, TOP_W), (TOP_W * TOPS // 4) ** -0.5, 0.0625, ((0, 8), (1, 8)))
    parent_leaf = draw_parent_leaf(jax.random.fold_in(arg_keys[19], 71), 0)
    parent_mid = draw_parent_mid(jax.random.fold_in(arg_keys[19], 71), 0)
    width_leaf = jax.vmap(lambda own: ragged_sizes(own, LEAVES, LEAVES * LEAF_W * 3 // 4, LEAF_W, 0))(jax.random.split(arg_keys[14], N_GZ)).reshape((N_GZ, LEAVES)).astype(jnp.int32)
    width_mid = jax.vmap(lambda own: ragged_sizes(own, MIDS, MIDS * MID_W * 3 // 4, MID_W, 0))(jax.random.split(arg_keys[15], N_GZ)).reshape((N_GZ, MIDS)).astype(jnp.int32)
    width_top = ragged_sizes(arg_keys[16], TOPS, TOPS * TOP_W * 3 // 4, TOP_W, 0).astype(jnp.int32)
    pattern_leaf = touch_ends((jax.random.randint(arg_keys[17], (N_GZ, LEAVES, 2), 0, 4) < 3).astype(jnp.int32), jax.random.fold_in(arg_keys[17], 1), 0, 1)
    pattern_mid = touch_ends((jax.random.randint(arg_keys[18], (N_GZ, MIDS), 0, 4) < 3).astype(jnp.int32), jax.random.fold_in(arg_keys[18], 1), 0, 1)
    return dict(rhs_leaf=rhs_leaf, rhs_mid=rhs_mid, rhs_top=rhs_top, inv_leaf=inv_leaf, inv_mid=inv_mid, inv_top=inv_top, off_leaf_mid=off_leaf_mid, off_leaf_top=off_leaf_top, off_leaf_out=off_leaf_out, off_mid_top=off_mid_top, off_mid_out=off_mid_out, off_top_out=off_top_out, parent_leaf=parent_leaf, parent_mid=parent_mid, width_leaf=width_leaf, width_mid=width_mid, width_top=width_top, pattern_leaf=pattern_leaf, pattern_mid=pattern_mid)


def solve_blocks(inverse, right_side, widths):
    matrix_product = jnp.einsum("kpw,kwr->kpr", inverse.astype(jnp.float32), right_side.astype(jnp.float32))
    row_ids = jnp.arange(inverse.shape[1], dtype=jnp.int32)
    active_mask = row_ids[None, :, None] < widths[:, None, None]
    return jnp.where(active_mask, matrix_product, jnp.float32(0.0)).astype(jnp.bfloat16)


def apply_blocks(matrix, solved):
    return jnp.einsum("kmw,kwr->kmr", matrix.astype(jnp.float32), solved.astype(jnp.float32))


def outer_term(matrix, solved, flags):
    return jnp.einsum("k,kmw,kwr->mr", flags, matrix.astype(jnp.float32), solved.astype(jnp.float32))


def reference(rhs_leaf, rhs_mid, rhs_top, inv_leaf, inv_mid, inv_top, off_leaf_mid, off_leaf_top, off_leaf_out, off_mid_top, off_mid_out, off_top_out, parent_leaf, parent_mid, width_leaf, width_mid, width_top, pattern_leaf, pattern_mid):
    top_sums = jnp.zeros((TOPS, TOP_W, RHS), jnp.float32)
    outer_sum = jnp.zeros((OUTER_ROWS, RHS), jnp.float32)
    leaf_list = []
    mid_list = []
    for layer_idx in range(N_GZ):
        leaf_x = solve_blocks(inv_leaf[layer_idx], rhs_leaf[layer_idx], width_leaf[layer_idx])
        leaf_parent = parent_leaf[layer_idx, :, 0]
        mid_parents = parent_mid[layer_idx, :, 0]
        grand_parent = mid_parents[leaf_parent]
        leaf_flags = pattern_leaf[layer_idx].astype(jnp.float32)
        mid_sums = jax.ops.segment_sum(apply_blocks(off_leaf_mid[layer_idx], leaf_x), leaf_parent, num_segments=MIDS)
        leaf_upward = apply_blocks(off_leaf_top[layer_idx], leaf_x) * leaf_flags[:, 0, None, None]
        top_sums = top_sums + jax.ops.segment_sum(leaf_upward, grand_parent, num_segments=TOPS)
        outer_sum = outer_sum + outer_term(off_leaf_out[layer_idx], leaf_x, leaf_flags[:, 1])
        mid_input = (rhs_mid[layer_idx].astype(jnp.float32) - mid_sums).astype(jnp.bfloat16)
        mid_x = solve_blocks(inv_mid[layer_idx], mid_input, width_mid[layer_idx])
        top_sums = top_sums + jax.ops.segment_sum(apply_blocks(off_mid_top[layer_idx], mid_x), mid_parents, num_segments=TOPS)
        outer_sum = outer_sum + outer_term(off_mid_out[layer_idx], mid_x, pattern_mid[layer_idx].astype(jnp.float32))
        leaf_list.append(leaf_x)
        mid_list.append(mid_x)
    top_input = (rhs_top.astype(jnp.float32) - top_sums).astype(jnp.bfloat16)
    top_x = solve_blocks(inv_top, top_input, width_top)
    outer_sum = outer_sum + outer_term(off_top_out, top_x, jnp.ones((TOPS,), jnp.float32))
    return jnp.stack(leaf_list), jnp.stack(mid_list), top_x, outer_sum
```

```python
import functools

import jax
import jax.numpy as jnp
from jax import lax
from jax.experimental import pallas as pl
from jax.experimental.pallas import tpu as pltpu
from jax.sharding import PartitionSpec as P

MESH_IDS = pl.DeviceIdType.MESH
F32 = jnp.float32
BF16 = jnp.bfloat16
LANES = 128


def dot(a, b):
    return jnp.dot(a, b, preferred_element_type=F32)


def live_rows(values, first_row, width):
    row_ids = first_row + lax.broadcasted_iota(jnp.int32, values.shape, 0)
    return jnp.where(row_ids < width, values, 0.0)


def flagged(values, flag):
    return jnp.where(flag != 0, values, jnp.zeros_like(values))


def subtree_kernel(
    parent_leaf, parent_mid, width_leaf, width_mid, pattern_leaf,
    rhs_leaf, inv_leaf, off_leaf_mid, rhs_mid, inv_mid, off_leaf_top, off_mid_top,
    leaf_out, mid_out, top_out,
    rl, il, lm, rm, im, lt, mt, xl, xm, top, load_sems, store_sems,
):
    leaves, mids, tops = xl.shape[0], xm.shape[0], top.shape[0]
    loads = [
        pltpu.make_async_copy(src.at[0], dst, load_sems.at[i])
        for i, (src, dst) in enumerate((
            (inv_leaf, il), (rhs_leaf, rl), (off_leaf_mid, lm), (inv_mid, im), (rhs_mid, rm),
            (off_leaf_top, lt), (off_mid_top, mt),
        ))
    ]
    for load in loads:
        load.start()

    def clear(s, carry):
        top[s] = jnp.zeros(top.shape[1:], top.dtype)
        return carry

    lax.fori_loop(0, tops, clear, 0)

    parents = [lax.rem(parent_leaf[0, k], mids) for k in range(leaves)]
    first, last = [], []
    for j in range(mids):
        low = jnp.int32(0)
        high = jnp.int32(0)
        for k in range(leaves):
            high = jnp.where(parents[k] == j, k, high)
            back = leaves - 1 - k
            low = jnp.where(parents[back] == j, back, low)
        first.append(low)
        last.append(high)

    loads[0].wait()
    loads[1].wait()
    for k in range(leaves):
        xl[k] = live_rows(dot(il[k], rl[k]), 0, width_leaf[0, k]).astype(BF16)
    store_leaf = pltpu.make_async_copy(xl, leaf_out.at[0], store_sems.at[0])
    store_leaf.start()

    for load in loads[2:5]:
        load.wait()
    for j in range(mids):
        total = dot(lm[first[j]], xl[first[j]]) + dot(lm[last[j]], xl[last[j]])
        mid_input = (rm[j].astype(F32) - total).astype(BF16)
        xm[j] = live_rows(dot(im[j], mid_input), 0, width_mid[0, j]).astype(BF16)
    store_mid = pltpu.make_async_copy(xm, mid_out.at[0], store_sems.at[1])
    store_mid.start()

    for load in loads[5:]:
        load.wait()
    for j in range(mids):
        low, high = first[j], last[j]
        update = dot(mt[j], xm[j])
        update += dot(lt[low], flagged(xl[low], pattern_leaf[0, low]))
        update += dot(lt[high], flagged(xl[high], pattern_leaf[0, high]))
        s = lax.rem(parent_mid[0, j], tops)
        top[s] = (top[s].astype(F32) + update).astype(BF16)
    store_top = pltpu.make_async_copy(top, top_out, store_sems.at[2])
    store_top.start()
    store_leaf.wait()
    store_mid.wait()
    store_top.wait()


def upper_kernel(
    nz, nx, ny,
    width_top, pattern_leaf, pattern_mid,
    updates, leaf_x, mid_x, off_leaf_out, off_mid_out, rhs_top, inv_top, off_top_out,
    top_solution, outer_out,
    t_own, t_rx, t_sum, a_rx, b_rx, a_sum, b_sum, a_rx2, b_rx2, top_in, inv, rhs, solved, sol_v,
    xl, xm, ol, om, ot,
    o_t, o_rx, o_s, o_rz, o_z, o_rx2, o_x, o_ry, o_fin,
    q_t, q_ry, q_z, q_rz, out_v,
    load_sems, core_s, core_r, pre_s, pre_r, a_s, a_r, b_s, b_r, a2_s, a2_r, b2_s, b2_r,
    g_s, g_r, f_s, f_r, oz_s, oz_r, ox_s, ox_r, oy_s, oy_r, qy_s, qy_r, qz_s, qz_r,
):
    z = lax.axis_index("pr")
    pc = lax.axis_index("pc")
    y = lax.axis_index("gz")
    x = pc // 2
    c = pc % 2
    other = 1 - c
    sibling = 2 * x + other
    tops = rhs_top.shape[0]
    per_y = tops // ny
    half = t_own.shape[3] // LANES
    slab = rhs_top.shape[1]
    part = t_own.shape[2]
    half_rows = 2 * part
    chunk = q_z.shape[1]
    rows = outer_out.shape[1]
    wide = o_t.shape[3]

    def to(z_, pc_, y_):
        return (z_, pc_, y_)

    def remote(src, dst, send, recv, device):
        return pltpu.make_async_remote_copy(
            src_ref=src, dst_ref=dst, send_sem=send, recv_sem=recv,
            device_id=device, device_id_type=MESH_IDS,
        )

    barrier = pltpu.get_barrier_semaphore()
    partners = [to(z, lax.rem(pc + d, 2 * nx), y) for d in range(1, 2 * nx)]
    partners += [to(z, pc, lax.rem(y + d, ny)) for d in range(1, ny)]
    partners += [to(lax.rem(z + d, nz), pc, y) for d in range(1, nz)]
    for partner in partners:
        pl.semaphore_signal(barrier, inc=1, device_id=partner, device_id_type=MESH_IDS)

    own_first = pl.multiple_of(c * half_rows, half_rows)
    load_pairs = [
        (updates.at[:, pl.ds(pl.multiple_of(c * half_rows + p * part, part), part), :], t_own.at[p])
        for p in range(2)
    ] + [
        (leaf_x.at[0], xl), (mid_x.at[0], xm), (off_leaf_out.at[0], ol), (off_mid_out.at[0], om),
        (off_top_out.at[pl.ds(y * per_y, per_y)], ot),
    ]
    loads = [
        pltpu.make_async_copy(src, dst, load_sems.at[i]) for i, (src, dst) in enumerate(load_pairs)
    ]
    for i in (2, 3, 0, 4, 5, 1, 6):
        loads[i].start()
    pl.semaphore_wait(barrier, len(partners))

    core_copies = [
        remote(
            updates.at[:, pl.ds(pl.multiple_of(other * half_rows + p * part, part), part), :],
            t_rx.at[p], core_s.at[p], core_r.at[p], to(z, sibling, y),
        )
        for p in range(2)
    ]
    for copy in core_copies:
        copy.start()

    slot = lax.rem(pc, nx)
    target_core = pc // nx
    pre_copies = []
    for d in range(nx):
        tx = lax.rem(x + d, nx)
        s = y * per_y + tx // half
        column = pl.multiple_of(lax.rem(tx, half) * LANES, LANES)
        pairs = (
            (inv_top.at[s], inv.at[slot]),
            (rhs_top.at[s, :, pl.ds(column, LANES)], rhs.at[slot]),
        )
        for i, (src, dst) in enumerate(pairs):
            copy = remote(
                src, dst, pre_s.at[i, d], pre_r.at[i, slot], to(z, 2 * tx + target_core, y)
            )
            pre_copies.append((d, copy))
            if d == 0:
                @pl.when(target_core == c)
                def _():
                    pltpu.make_async_copy(src, dst, pre_r.at[i, slot]).start()

                @pl.when(target_core != c)
                def _():
                    copy.start()
            else:
                copy.start()

    loads[2].wait()
    loads[3].wait()
    for k in range(xl.shape[0]):
        xl[k] = flagged(xl[k], pattern_leaf[1, k])
    for j in range(xm.shape[0]):
        xm[j] = flagged(xm[j], pattern_mid[0, j])
    loads[4].wait()
    loads[5].wait()

    def outer_rows(i, carry):
        first = pl.multiple_of(i * 2 * rows, 2 * rows)
        block = pl.ds(first, 2 * rows)
        total = jnp.zeros((2 * rows, xl.shape[2]), F32)
        for k in range(xl.shape[0]):
            total += dot(ol[k, block, :], xl[k])
        for j in range(xm.shape[0]):
            total += dot(om[j, block, :], xm[j])
        for core in range(2):
            turned = total[core * rows:(core + 1) * rows].T
            o_t[core, i] = turned.reshape(nz, wide, rows).astype(BF16)
        return carry

    lax.fori_loop(0, nx // 2, outer_rows, 0)

    a_copies, b_copies = [], []
    for p in range(2):
        loads[p].wait()
        core_copies[p].wait_recv()

        def pair_sum(s, carry):
            total = (t_own[p, s].astype(F32) + t_rx[p, s].astype(F32)).astype(BF16)
            for h in range(half):
                t_sum[p, s // per_y, (s % per_y) * half + h] = total[:, h * LANES:(h + 1) * LANES]
            return carry

        lax.fori_loop(0, tops, pair_sum, 0)
        if p == 0:
            for d in range(1, nx):
                tx = lax.rem(x + d, nx)
                a_copies.append(remote(
                    t_sum.at[0, :, tx], a_rx.at[d - 1], a_s.at[d - 1], a_r.at[d - 1],
                    to(z, 2 * tx + c, y),
                ))
                a_copies[-1].start()
        else:
            for d in range(1, ny):
                ty = lax.rem(y + d, ny)
                b_copies.append(remote(
                    t_sum.at[1, ty], b_rx.at[d - 1], b_s.at[d - 1], b_r.at[d - 1], to(z, pc, ty),
                ))
                b_copies[-1].start()

    lax.fori_loop(nx // 2, nx, outer_rows, 0)
    o_core = remote(
        o_t.at[other], o_rx, core_s.at[2], core_r.at[2], to(z, sibling, y)
    )
    o_core.start()

    a2_copies, b2_copies = [], []
    for copy in a_copies:
        copy.wait_recv()
    for i in range(ny):
        total = t_sum[0, i, x].astype(F32)
        for d in range(nx - 1):
            total += a_rx[d, i].astype(F32)
        a_sum[i] = total.astype(BF16)
    for d in range(1, ny):
        ty = lax.rem(y + d, ny)
        a2_copies.append(remote(
            a_sum.at[ty], a_rx2.at[d - 1], a2_s.at[d - 1], a2_r.at[d - 1], to(z, pc, ty),
        ))
        a2_copies[-1].start()
    for copy in b_copies:
        copy.wait_recv()
    for i in range(nx):
        total = t_sum[1, y, i].astype(F32)
        for d in range(ny - 1):
            total += b_rx[d, i].astype(F32)
        b_sum[i] = total.astype(BF16)
    for d in range(1, nx):
        tx = lax.rem(x + d, nx)
        b2_copies.append(remote(
            b_sum.at[tx], b_rx2.at[d - 1], b2_s.at[d - 1], b2_r.at[d - 1], to(z, 2 * tx + c, y),
        ))
        b2_copies[-1].start()

    o_core.wait_recv()
    oz_copies = []

    def outer_pair(i, carry):
        o_s[i] = (o_t[c, i].astype(F32) + o_rx[i].astype(F32)).astype(BF16)
        return carry

    lax.fori_loop(0, nx, outer_pair, 0)
    for d in range(1, nz):
        tz = lax.rem(z + d, nz)
        oz_copies.append(remote(
            o_s.at[:, tz], o_rz.at[d - 1], oz_s.at[d - 1], oz_r.at[d - 1], to(tz, pc, y),
        ))
        oz_copies[-1].start()

    for i in range(nx):
        pre = [
            remote(inv_top.at[0], inv.at[i], pre_s.at[0, 0], pre_r.at[0, i], to(z, sibling, y)),
            remote(rhs_top.at[0, :, pl.ds(0, LANES)], rhs.at[i], pre_s.at[1, 0], pre_r.at[1, i],
                   to(z, sibling, y)),
        ]
        for copy in pre:
            copy.wait_recv()
    right = rhs[...].reshape(half_rows, LANES).astype(F32)
    for copy in a2_copies:
        copy.wait_recv()
    total = a_sum[y].astype(F32)
    for d in range(ny - 1):
        total += a_rx2[d].astype(F32)
    top_in[c, pl.ds(0, part), :] = (right[:part] - total).astype(BF16)
    for copy in b2_copies:
        copy.wait_recv()
    total = b_sum[x].astype(F32)
    for d in range(nx - 1):
        total += b_rx2[d].astype(F32)
    top_in[c, pl.ds(part, part), :] = (right[part:] - total).astype(BF16)
    in_copy = remote(top_in.at[c], top_in.at[c], core_s.at[3], core_r.at[3], to(z, sibling, y))
    in_copy.start()
    in_copy.wait_recv()

    block = dot(inv[...].reshape(half_rows, inv.shape[2]), top_in[...].reshape(2 * half_rows, LANES))
    width = width_top[y * per_y + x // half]
    solved[x, c] = live_rows(block, c * half_rows, width).astype(BF16)

    g_copies, f_copies = [], []
    for d in range(1, nx):
        tx = lax.rem(x + d, nx)
        g_copies.append(remote(
            solved.at[x, c], solved.at[x, c], g_s.at[d - 1], g_r.at[d - 1], to(z, 2 * tx + c, y),
        ))
        g_copies[-1].start()
    f_copies.append(remote(
        solved.at[x, c], solved.at[x, c], f_s.at[0], f_r.at[0], to(z, sibling, y)
    ))
    f_copies[-1].start()

    for copy in oz_copies:
        copy.wait_recv()
    ox_copies = []
    for i in range(nx):
        total = o_s[i, z].astype(F32)
        for d in range(nz - 1):
            total += o_rz[d, i].astype(F32)
        o_z[i] = total.astype(BF16)
    for d in range(1, nx):
        tx = lax.rem(x + d, nx)
        ox_copies.append(remote(
            o_z.at[tx], o_rx2.at[d - 1], ox_s.at[d - 1], ox_r.at[d - 1], to(z, 2 * tx + c, y),
        ))
        ox_copies[-1].start()

    for d in range(1, nx):
        sx = lax.rem(x + nx - d, nx)
        g_copies[d - 1].wait_recv()
        f_copies.append(remote(
            solved.at[sx, c], solved.at[sx, c], f_s.at[d], f_r.at[d], to(z, sibling, y)
        ))
        f_copies[-1].start()

    for copy in ox_copies:
        copy.wait_recv()
    total = o_z[x].astype(F32)
    for d in range(nx - 1):
        total += o_rx2[d].astype(F32)
    o_x[...] = total.reshape(ny, chunk, rows)
    oy_copies = []
    for d in range(1, ny):
        ty = lax.rem(y + d, ny)
        oy_copies.append(remote(
            o_x.at[ty], o_ry.at[d - 1], oy_s.at[d - 1], oy_r.at[d - 1], to(z, pc, ty),
        ))
        oy_copies[-1].start()

    loads[6].wait()
    for copy in f_copies:
        copy.wait_recv()

    total = jnp.zeros((rows, half * LANES), F32)
    for t in range(per_y):
        blocks = [
            solved[t * half + h].reshape(2 * half_rows, LANES) for h in range(half)
        ]
        total += dot(ot[t], jnp.concatenate(blocks, axis=1))
    turned = total.T.reshape(nz, ny, chunk, rows)
    for i in range(ny):
        q_t[i] = turned[:, i].reshape(nz * chunk, rows).astype(BF16)
    qy_copies = []
    for d in range(1, ny):
        ty = lax.rem(y + d, ny)
        qy_copies.append(remote(
            q_t.at[ty], q_ry.at[d - 1], qy_s.at[d - 1], qy_r.at[d - 1], to(z, pc, ty),
        ))
        qy_copies[-1].start()

    for t in range(per_y):
        for h in range(half):
            sol_v[t, :, h * LANES:(h + 1) * LANES] = solved[
                t * half + h, pc // nx, pl.ds(pl.multiple_of(slot * slab, slab), slab), :
            ]
    store = pltpu.make_async_copy(sol_v, top_solution, load_sems.at[7])
    store.start()
    for copy in oy_copies:
        copy.wait_recv()
    total = o_x[y]
    for d in range(ny - 1):
        total += o_ry[d]
    o_fin[...] = total

    for copy in qy_copies:
        copy.wait_recv()
    total = q_t[y].astype(F32)
    for d in range(ny - 1):
        total += q_ry[d].astype(F32)
    q_z[...] = total.reshape(nz, chunk, rows)
    qz_copies = []
    for d in range(1, nz):
        tz = lax.rem(z + d, nz)
        qz_copies.append(remote(
            q_z.at[tz], q_rz.at[d - 1], qz_s.at[d - 1], qz_r.at[d - 1], to(tz, pc, y),
        ))
        qz_copies[-1].start()
    for copy in (
        core_copies + [o_core, in_copy] + a_copies + b_copies + a2_copies + b2_copies
        + g_copies + f_copies + oz_copies + ox_copies + oy_copies + qy_copies
    ):
        copy.wait_send()
    for d, copy in pre_copies:
        if d == 0:
            @pl.when(target_core != c)
            def _():
                copy.wait_send()
        else:
            copy.wait_send()
    store.wait()
    for copy in qz_copies:
        copy.wait_recv()
    total = q_z[z] + o_fin[...]
    for d in range(nz - 1):
        total += q_rz[d]
    out_v[...] = total
    last = pltpu.make_async_copy(out_v, outer_out, load_sems.at[8])
    last.start()
    for copy in qz_copies:
        copy.wait_send()
    last.wait()


def on_device(
    nz, nx, ny,
    rhs_leaf, rhs_mid, rhs_top, inv_leaf, inv_mid, inv_top,
    off_leaf_mid, off_leaf_top, off_leaf_out, off_mid_top, off_mid_out, off_top_out,
    parent_leaf, parent_mid, width_leaf, width_mid, width_top, pattern_leaf, pattern_mid,
):
    smem = pl.BlockSpec(memory_space=pltpu.SMEM)
    hbm = pl.BlockSpec(memory_space=pl.ANY)
    leaves, leaf_w, num_rhs = rhs_leaf.shape[1:]
    mids, mid_w = rhs_mid.shape[1:3]
    tops, slab = rhs_top.shape[:2]
    top_w = inv_top.shape[2]
    outer = off_leaf_out.shape[2]
    rows = off_top_out.shape[1]
    half = num_rhs // LANES
    per_y = tops // ny
    assert per_y * half == nx and slab * 2 * nx == top_w and rows * 2 * nx == outer
    pattern = jnp.transpose(pattern_leaf[0], (1, 0))
    parents_l = parent_leaf.reshape(1, leaves)
    parents_m = parent_mid.reshape(1, mids)

    def vm(*shape, dtype=BF16):
        return pltpu.VMEM(shape, dtype)

    leaf_x, mid_x, updates = pl.pallas_call(
        subtree_kernel,
        out_shape=(
            jax.ShapeDtypeStruct(rhs_leaf.shape, BF16),
            jax.ShapeDtypeStruct(rhs_mid.shape, BF16),
            jax.ShapeDtypeStruct((tops, top_w, num_rhs), BF16),
        ),
        in_specs=[smem] * 5 + [hbm] * 7,
        out_specs=(hbm,) * 3,
        scratch_shapes=[
            vm(leaves, leaf_w, num_rhs), vm(leaves, leaf_w, leaf_w), vm(leaves, mid_w, leaf_w),
            vm(mids, mid_w, num_rhs), vm(mids, mid_w, mid_w),
            vm(leaves, top_w, leaf_w), vm(mids, top_w, mid_w),
            vm(leaves, leaf_w, num_rhs), vm(mids, mid_w, num_rhs), vm(tops, top_w, num_rhs),
            pltpu.SemaphoreType.DMA((7,)), pltpu.SemaphoreType.DMA((3,)),
        ],
        compiler_params=pltpu.CompilerParams(vmem_limit_bytes=60 << 20),
        name="subtrees",
    )(
        parents_l, parents_m, width_leaf, width_mid, pattern,
        rhs_leaf, inv_leaf, off_leaf_mid, rhs_mid, inv_mid, off_leaf_top, off_mid_top,
    )

    half_rows = top_w // 2
    part = half_rows // 2
    wide = num_rhs // nz
    chunk = wide // ny
    sems = pltpu.SemaphoreType.DMA
    top_solution, outer_part = pl.pallas_call(
        functools.partial(upper_kernel, nz, nx, ny),
        out_shape=(
            jax.ShapeDtypeStruct((per_y, slab, num_rhs), BF16),
            jax.ShapeDtypeStruct((chunk, rows), F32),
        ),
        in_specs=[smem] * 3 + [hbm] * 8,
        out_specs=(hbm, hbm),
        scratch_shapes=[
            vm(2, tops, part, num_rhs), vm(2, tops, part, num_rhs),
            vm(2, ny, nx, part, LANES),
            vm(nx - 1, ny, part, LANES), vm(ny - 1, nx, part, LANES),
            vm(ny, part, LANES), vm(nx, part, LANES),
            vm(ny - 1, part, LANES), vm(nx - 1, part, LANES),
            vm(2, half_rows, LANES), vm(nx, slab, top_w), vm(nx, slab, LANES),
            vm(nx, 2, half_rows, LANES), vm(per_y, slab, num_rhs),
            vm(leaves, leaf_w, num_rhs), vm(mids, mid_w, num_rhs),
            vm(leaves, outer, leaf_w), vm(mids, outer, mid_w), vm(per_y, rows, top_w),
            vm(2, nx, nz, wide, rows), vm(nx, nz, wide, rows), vm(nx, nz, wide, rows),
            vm(nz - 1, nx, wide, rows), vm(nx, wide, rows), vm(nx - 1, wide, rows),
            vm(ny, chunk, rows, dtype=F32), vm(ny - 1, chunk, rows, dtype=F32),
            vm(chunk, rows, dtype=F32),
            vm(ny, nz * chunk, rows), vm(ny - 1, nz * chunk, rows),
            vm(nz, chunk, rows, dtype=F32), vm(nz - 1, chunk, rows, dtype=F32),
            vm(chunk, rows, dtype=F32),
            sems((9,)), sems((4,)), sems((4,)), sems((2, nx)), sems((2, nx)),
            sems((nx - 1,)), sems((nx - 1,)), sems((ny - 1,)), sems((ny - 1,)),
            sems((ny - 1,)), sems((ny - 1,)), sems((nx - 1,)), sems((nx - 1,)),
            sems((nx - 1,)), sems((nx - 1,)), sems((nx,)), sems((nx,)),
            sems((nz - 1,)), sems((nz - 1,)), sems((nx - 1,)), sems((nx - 1,)),
            sems((ny - 1,)), sems((ny - 1,)), sems((ny - 1,)), sems((ny - 1,)),
            sems((nz - 1,)), sems((nz - 1,)),
        ],
        compiler_params=pltpu.CompilerParams(
            collective_id=0, has_side_effects=True, vmem_limit_bytes=60 << 20
        ),
        name="upper",
    )(
        width_top, pattern, pattern_mid,
        updates, leaf_x, mid_x, off_leaf_out, off_mid_out, rhs_top, inv_top, off_top_out,
    )
    return leaf_x, mid_x, top_solution, outer_part.T


def solution(mesh):
    sizes = dict(mesh.shape)
    deep = P("gz", ("pr", "pc"), None, None)
    flat = P("pr", "pc", None)
    return jax.shard_map(
        functools.partial(on_device, sizes["pr"], sizes["pc"] // 2, sizes["gz"]),
        mesh=mesh,
        in_specs=(
            deep, deep, flat, deep, deep, flat,
            deep, deep, deep, deep, deep, flat,
            P("gz", ("pr", "pc"), None),
            P("gz", ("pr", "pc"), None),
            P("gz", ("pr", "pc")),
            P("gz", ("pr", "pc")),
            P("pr"),
            P("gz", ("pr", "pc"), None),
            P("gz", ("pr", "pc")),
        ),
        out_specs=(deep, deep, P(("pr", "gz"), "pc", None), P("pc", ("pr", "gz"))),
        check_vma=False,
    )
```

```python
import functools

import jax
import jax.numpy as jnp
from jax import lax
from jax.experimental import pallas as pl
from jax.experimental.pallas import tpu as pltpu
from jax.sharding import PartitionSpec as P

MESH_IDS = pl.DeviceIdType.MESH
F32 = jnp.float32
BF16 = jnp.bfloat16
LANES = 128


def dot(a, b):
    return jnp.dot(a, b, preferred_element_type=F32)


def live_rows(values, first_row, width):
    row_ids = first_row + lax.broadcasted_iota(jnp.int32, values.shape, 0)
    return jnp.where(row_ids < width, values, 0.0)


def flagged(values, flag):
    return jnp.where(flag != 0, values, jnp.zeros_like(values))


def dot_nt(a, b):
    return lax.dot_general(a, b, (((1,), (1,)), ((), ())), preferred_element_type=F32)


def window_kernel(
    nz, nx, ny,
    parent_leaf, parent_mid, width_leaf, width_mid, width_top, pattern_leaf, pattern_mid,
    rhs_leaf, rhs_mid, rhs_top, inv_leaf, inv_mid, inv_top,
    off_leaf_mid, off_leaf_top, off_leaf_out, off_mid_top, off_mid_out, off_top_out,
    leaf_out, mid_out, top_solution, outer_out,
    rl, il, lm, rm, im, lt, mt, xl, xm, ol, om, xo, up_own, up_rx, mask, mask_rx,
    t_sum, a_rx, b_rx, a_sum, b_sum, a_rx2, b_rx2, top_in, inv, rhs,
    unit, sol_rx, sol_v, turned, gathered, wt,
    o_t, o_rx, o_s, o_rz, o_z, o_rx2, o_x, o_ry, o_fin, q, q_rx, out_v,
    load_sems, store_sems, core_s, core_r, pre_s, pre_r, a_s, a_r, b_s, b_r, a2_s, a2_r, b2_s, b2_r,
    sol_s, sol_r, g_s, g_r, oz_s, oz_r, ox_s, ox_r, oy_s, oy_r, q_s, q_r,
):
    z = lax.axis_index("pr")
    pc = lax.axis_index("pc")
    y = lax.axis_index("gz")
    x = pc // 2
    c = pc % 2
    other = 1 - c
    sibling = 2 * x + other
    leaves, mids = xl.shape[0], xm.shape[0]
    tops = rhs_top.shape[0]
    per_y = tops // ny
    half = xl.shape[2] // LANES
    slab = rhs_top.shape[1]
    part = t_sum.shape[3]
    half_rows = 2 * part
    chunk = q.shape[2]
    rows = outer_out.shape[1]
    wide = o_t.shape[3]
    group = gathered.shape[2]
    num_rhs = xl.shape[2]

    def remote(src, dst, send, recv, device):
        return pltpu.make_async_remote_copy(
            src_ref=src, dst_ref=dst, send_sem=send, recv_sem=recv,
            device_id=device, device_id_type=MESH_IDS,
        )

    barrier = pltpu.get_barrier_semaphore()
    partners = [(z, lax.rem(pc + d, 2 * nx), y) for d in range(1, 2 * nx)]
    for dy in range(1, ny):
        for dx in range(nx):
            partners.append((z, lax.rem(pc + 2 * dx, 2 * nx), lax.rem(y + dy, ny)))
    for dz in range(1, nz):
        for core in range(2):
            partners.append((lax.rem(z + dz, nz), 2 * x + core, y))
    for partner in partners:
        pl.semaphore_signal(barrier, inc=1, device_id=partner, device_id_type=MESH_IDS)

    load_pairs = [
        (inv_leaf.at[0], il), (rhs_leaf.at[0], rl), (off_leaf_mid.at[0], lm),
        (inv_mid.at[0], im), (rhs_mid.at[0], rm), (off_mid_top.at[0], mt), (off_leaf_top.at[0], lt),
        (off_leaf_out.at[0], ol), (off_mid_out.at[0], om),
        (off_top_out.at[:, :, pl.ds(pl.multiple_of(c * half_rows, half_rows), half_rows)], wt.at[:, c]),
    ]
    loads = [
        pltpu.make_async_copy(src, dst, load_sems.at[i]) for i, (src, dst) in enumerate(load_pairs)
    ]
    for load in loads[:7]:
        load.start()

    parents = [lax.rem(parent_leaf[0, k], mids) for k in range(leaves)]
    first, last = [], []
    for j in range(mids):
        low = jnp.int32(0)
        high = jnp.int32(0)
        for k in range(leaves):
            high = jnp.where(parents[k] == j, k, high)
            back = leaves - 1 - k
            low = jnp.where(parents[back] == j, back, low)
        first.append(low)
        last.append(high)
    for j in range(mids):
        ids = lax.broadcasted_iota(jnp.int32, mask.shape[1:], 0)
        mask[j] = jnp.where(ids == lax.rem(parent_mid[0, j], tops), 1.0, 0.0)

    loads[0].wait()
    loads[1].wait()
    for k in range(leaves):
        xl[k] = live_rows(dot(il[k], rl[k]), 0, width_leaf[0, k]).astype(BF16)
    store_leaf = pltpu.make_async_copy(xl, leaf_out.at[0], store_sems.at[0])
    store_leaf.start()

    for load in loads[2:5]:
        load.wait()
    for j in range(mids):
        total = dot(
            jnp.concatenate([lm[first[j]], lm[last[j]]], axis=1),
            jnp.concatenate([xl[first[j]], xl[last[j]]], axis=0),
        )
        mid_input = (rm[j].astype(F32) - total).astype(BF16)
        xm[j] = live_rows(dot(im[j], mid_input), 0, width_mid[0, j]).astype(BF16)
    store_mid = pltpu.make_async_copy(xm, mid_out.at[0], store_sems.at[1])
    store_mid.start()

    pl.semaphore_wait(barrier, len(partners))
    mask_copy = remote(mask, mask_rx, core_s.at[0], core_r.at[0], (z, sibling, y))
    mask_copy.start()

    slot = lax.rem(pc, nx)
    target_core = pc // nx
    pre_copies = []
    for d in range(nx):
        tx = lax.rem(x + d, nx)
        s = y * per_y + tx // half
        column = pl.multiple_of(lax.rem(tx, half) * LANES, LANES)
        pairs = (
            (inv_top.at[s], inv.at[slot]),
            (rhs_top.at[s, :, pl.ds(column, LANES)], rhs.at[slot]),
        )
        for i, (src, dst) in enumerate(pairs):
            copy = remote(
                src, dst, pre_s.at[i, d], pre_r.at[i, slot], (z, 2 * tx + target_core, y)
            )
            pre_copies.append((d, copy))
            if d == 0:
                @pl.when(target_core == c)
                def _():
                    pltpu.make_async_copy(src, dst, pre_r.at[i, slot]).start()

                @pl.when(target_core != c)
                def _():
                    copy.start()
            else:
                copy.start()

    loads[5].wait()
    loads[6].wait()
    up_copies = []
    for j in range(mids):
        low, high = first[j], last[j]
        update = dot(
            jnp.concatenate([mt[j], lt[low], lt[high]], axis=1),
            jnp.concatenate([
                xm[j], flagged(xl[low], pattern_leaf[0, low]), flagged(xl[high], pattern_leaf[0, high])
            ], axis=0),
        )
        up_own[j] = update.astype(BF16)
        up_copies.append(remote(
            up_own.at[j, pl.ds(pl.multiple_of(other * half_rows, half_rows), half_rows), :],
            up_rx.at[j], core_s.at[1 + j], core_r.at[1 + j], (z, sibling, y),
        ))
        up_copies[-1].start()
    for load in loads[7:]:
        load.start()
    w_copy = remote(
        off_top_out.at[:, :, pl.ds(pl.multiple_of(other * half_rows, half_rows), half_rows)],
        wt.at[:, c], core_s.at[1 + mids], core_r.at[1 + mids], (z, sibling, y),
    )

    mask_copy.wait_recv()
    for copy in up_copies:
        copy.wait_recv()
    step = 16
    a_copies, b_copies = [], []
    for p in range(2):
        def pair_sum(i, carry):
            at = pl.multiple_of(i * step, step)
            mine = pl.ds(pl.multiple_of(c * half_rows + p * part + at, step), step)
            theirs = pl.ds(pl.multiple_of(p * part + at, step), step)
            blocks = [up_own[j, mine, :].astype(F32) for j in range(mids)]
            blocks += [up_rx[j, theirs, :].astype(F32) for j in range(mids)]
            for s in range(tops):
                for h in range(half):
                    total = jnp.zeros((step, LANES), F32)
                    for j in range(2 * mids):
                        table = mask if j < mids else mask_rx
                        weight = table[j % mids, s:s + 1, :]
                        total += weight * blocks[j][:, h * LANES:(h + 1) * LANES]
                    t_sum[p, s // per_y, (s % per_y) * half + h, pl.ds(at, step), :] = total.astype(BF16)
            return carry

        lax.fori_loop(0, part // step, pair_sum, 0)
        if p == 0:
            for d in range(1, nx):
                tx = lax.rem(x + d, nx)
                a_copies.append(remote(
                    t_sum.at[0, :, tx], a_rx.at[d - 1], a_s.at[d - 1], a_r.at[d - 1],
                    (z, 2 * tx + c, y),
                ))
                a_copies[-1].start()
        else:
            for d in range(1, ny):
                ty = lax.rem(y + d, ny)
                b_copies.append(remote(
                    t_sum.at[1, ty], b_rx.at[d - 1], b_s.at[d - 1], b_r.at[d - 1], (z, pc, ty),
                ))
                b_copies[-1].start()
    w_copy.start()

    leaf_w, mid_w = xl.shape[1], xm.shape[1]
    for k in range(leaves):
        xo[k * leaf_w:(k + 1) * leaf_w] = flagged(xl[k], pattern_leaf[1, k])
    base = leaves * leaf_w
    for j in range(mids):
        xo[base + j * mid_w:base + (j + 1) * mid_w] = flagged(xm[j], pattern_mid[0, j])
    loads[7].wait()
    loads[8].wait()

    def outer_rows(i, carry):
        block = pl.ds(pl.multiple_of(i * 2 * rows, 2 * rows), 2 * rows)
        total = dot(
            jnp.concatenate(
                [ol[k, block, :] for k in range(leaves)] + [om[j, block, :] for j in range(mids)],
                axis=1,
            ),
            xo[...],
        )
        for core in range(2):
            across = total[core * rows:(core + 1) * rows].T
            o_t[core, i] = across.reshape(nz, wide, rows).astype(BF16)
        return carry

    lax.fori_loop(0, nx, outer_rows, 0)
    o_core = remote(
        o_t.at[other], o_rx, core_s.at[2 + mids], core_r.at[2 + mids], (z, sibling, y)
    )
    o_core.start()

    a2_copies, b2_copies = [], []
    for copy in a_copies:
        copy.wait_recv()
    for i in range(ny):
        total = t_sum[0, i, x].astype(F32)
        for d in range(nx - 1):
            total += a_rx[d, i].astype(F32)
        a_sum[i] = total.astype(BF16)
    for d in range(1, ny):
        ty = lax.rem(y + d, ny)
        a2_copies.append(remote(
            a_sum.at[ty], a_rx2.at[d - 1], a2_s.at[d - 1], a2_r.at[d - 1], (z, pc, ty),
        ))
        a2_copies[-1].start()
    for copy in b_copies:
        copy.wait_recv()
    for i in range(nx):
        total = t_sum[1, y, i].astype(F32)
        for d in range(ny - 1):
            total += b_rx[d, i].astype(F32)
        b_sum[i] = total.astype(BF16)
    for d in range(1, nx):
        tx = lax.rem(x + d, nx)
        b2_copies.append(remote(
            b_sum.at[tx], b_rx2.at[d - 1], b2_s.at[d - 1], b2_r.at[d - 1], (z, 2 * tx + c, y),
        ))
        b2_copies[-1].start()

    o_core.wait_recv()
    oz_copies = []

    def outer_pair(i, carry):
        o_s[i] = (o_t[c, i].astype(F32) + o_rx[i].astype(F32)).astype(BF16)
        return carry

    lax.fori_loop(0, nx, outer_pair, 0)
    for d in range(1, nz):
        tz = lax.rem(z + d, nz)
        oz_copies.append(remote(
            o_s.at[:, tz], o_rz.at[d - 1], oz_s.at[d - 1], oz_r.at[d - 1], (tz, pc, y),
        ))
        oz_copies[-1].start()

    for i in range(nx):
        pre = [
            remote(inv_top.at[0], inv.at[i], pre_s.at[0, 0], pre_r.at[0, i], (z, sibling, y)),
            remote(rhs_top.at[0, :, pl.ds(0, LANES)], rhs.at[i], pre_s.at[1, 0], pre_r.at[1, i],
                   (z, sibling, y)),
        ]
        for copy in pre:
            copy.wait_recv()
    right = rhs[...].reshape(half_rows, LANES).astype(F32)
    for copy in a2_copies:
        copy.wait_recv()
    total = a_sum[y].astype(F32)
    for d in range(ny - 1):
        total += a_rx2[d].astype(F32)
    top_in[c, pl.ds(0, part), :] = (right[:part] - total).astype(BF16)
    for copy in b2_copies:
        copy.wait_recv()
    total = b_sum[x].astype(F32)
    for d in range(nx - 1):
        total += b_rx2[d].astype(F32)
    top_in[c, pl.ds(part, part), :] = (right[part:] - total).astype(BF16)
    in_copy = remote(
        top_in.at[c], top_in.at[c], core_s.at[3 + mids], core_r.at[3 + mids], (z, sibling, y)
    )
    in_copy.start()
    in_copy.wait_recv()

    block = dot(inv[...].reshape(half_rows, inv.shape[2]), top_in[...].reshape(2 * half_rows, LANES))
    block = live_rows(block, c * half_rows, width_top[y * per_y + x // half])
    across = block.T.reshape(nz // half, ny, chunk, half_rows)
    for i in range(ny):
        turned[i] = across[:, i].reshape(group, half_rows).astype(BF16)
    unit[...] = block.reshape(nx, slab, LANES).astype(BF16)

    g_copies = []
    for dy in range(ny):
        for dx in range(nx):
            if dx or dy:
                tx = lax.rem(x + dx, nx)
                ty = lax.rem(y + dy, ny)
                i = dy * nx + dx - 1
                g_copies.append(remote(
                    turned.at[ty], gathered.at[y, x], g_s.at[i], g_r.at[i], (z, 2 * tx + c, ty),
                ))
                g_copies[-1].start()
    gathered[y, x] = turned[y]

    sol_copies = []
    for d in range(nx):
        i = lax.rem(slot + d, nx)
        copy = remote(
            unit.at[i], sol_rx.at[x], sol_s.at[d], sol_r.at[x], (z, nx * c + i, y)
        )
        sol_copies.append((d, copy))
        if d == 0:
            @pl.when(target_core == c)
            def _():
                pltpu.make_async_copy(unit.at[i], sol_rx.at[x], sol_r.at[x]).start()

            @pl.when(target_core != c)
            def _():
                copy.start()
        else:
            copy.start()

    for copy in oz_copies:
        copy.wait_recv()
    ox_copies = []
    for i in range(nx):
        total = o_s[i, z].astype(F32)
        for d in range(nz - 1):
            total += o_rz[d, i].astype(F32)
        o_z[i] = total.astype(BF16)
    for d in range(1, nx):
        tx = lax.rem(x + d, nx)
        ox_copies.append(remote(
            o_z.at[tx], o_rx2.at[d - 1], ox_s.at[d - 1], ox_r.at[d - 1], (z, 2 * tx + c, y),
        ))
        ox_copies[-1].start()

    loads[9].wait()
    w_copy.wait_recv()
    for copy in g_copies:
        copy.wait_recv()

    total = jnp.zeros((half * group, 2 * rows), F32)
    for i in range(ny):
        for t in range(per_y):
            left = gathered[i, t * half:(t + 1) * half].reshape(half * group, half_rows)
            total += dot_nt(left, wt[i * per_y + t].reshape(2 * rows, half_rows))
    for core in range(2):
        q[core] = total[:, core * rows:(core + 1) * rows].reshape(nz, chunk, rows)
    q_copies = []
    for dz in range(nz):
        for dc in range(2):
            if dz or dc:
                tz = lax.rem(z + dz, nz)
                tc = lax.rem(c + dc, 2)
                i = 2 * dz + dc - 1
                q_copies.append(remote(
                    q.at[tc, tz], q_rx.at[i], q_s.at[i], q_r.at[i], (tz, 2 * x + tc, y),
                ))
                q_copies[-1].start()

    for copy in ox_copies:
        copy.wait_recv()
    total = o_z[x].astype(F32)
    for d in range(nx - 1):
        total += o_rx2[d].astype(F32)
    o_x[...] = total.reshape(ny, chunk, rows)
    oy_copies = []
    for d in range(1, ny):
        ty = lax.rem(y + d, ny)
        oy_copies.append(remote(
            o_x.at[ty], o_ry.at[d - 1], oy_s.at[d - 1], oy_r.at[d - 1], (z, pc, ty),
        ))
        oy_copies[-1].start()
    for i in range(nx):
        remote(unit.at[0], sol_rx.at[i], sol_s.at[0], sol_r.at[i], (z, sibling, y)).wait_recv()
    for t in range(per_y):
        for h in range(half):
            sol_v[t, :, h * LANES:(h + 1) * LANES] = sol_rx[t * half + h]
    store_sol = pltpu.make_async_copy(sol_v, top_solution, store_sems.at[2])
    store_sol.start()
    for copy in oy_copies:
        copy.wait_recv()
    total = o_x[y]
    for d in range(ny - 1):
        total += o_ry[d]
    o_fin[...] = total

    for copy in (
        [mask_copy, w_copy, o_core, in_copy] + up_copies + a_copies + b_copies + a2_copies
        + b2_copies + g_copies + oz_copies + ox_copies + oy_copies
    ):
        copy.wait_send()
    for d, copy in pre_copies + sol_copies:
        if d == 0:
            @pl.when(target_core != c)
            def _():
                copy.wait_send()
        else:
            copy.wait_send()
    store_leaf.wait()
    store_mid.wait()
    store_sol.wait()
    for copy in q_copies:
        copy.wait_recv()
    total = q[c, z] + o_fin[...]
    for d in range(2 * nz - 1):
        total += q_rx[d]
    out_v[...] = total
    last_store = pltpu.make_async_copy(out_v, outer_out, store_sems.at[3])
    last_store.start()
    for copy in q_copies:
        copy.wait_send()
    last_store.wait()


def finish_kernel(*refs):
    count = (len(refs) - 2) // 3
    ins, outs, held = refs[:count], refs[count:2 * count], refs[2 * count:3 * count]
    in_sems, out_sems = refs[-2:]
    loads = [
        pltpu.make_async_copy(ins[i], held[i], in_sems.at[i]) for i in range(count)
    ]
    stores = [
        pltpu.make_async_copy(held[i], outs[i], out_sems.at[i]) for i in range(count)
    ]
    for load in loads:
        load.start()
    for load, store in zip(loads, stores):
        load.wait()
        store.start()
    for store in stores:
        store.wait()


def on_device(
    nz, nx, ny,
    rhs_leaf, rhs_mid, rhs_top, inv_leaf, inv_mid, inv_top,
    off_leaf_mid, off_leaf_top, off_leaf_out, off_mid_top, off_mid_out, off_top_out,
    parent_leaf, parent_mid, width_leaf, width_mid, width_top, pattern_leaf, pattern_mid,
):
    smem = pl.BlockSpec(memory_space=pltpu.SMEM)
    hbm = pl.BlockSpec(memory_space=pl.ANY)
    leaves, leaf_w, num_rhs = rhs_leaf.shape[1:]
    mids, mid_w = rhs_mid.shape[1:3]
    tops, slab = rhs_top.shape[:2]
    top_w = inv_top.shape[2]
    outer = off_leaf_out.shape[2]
    rows = off_top_out.shape[1]
    half = num_rhs // LANES
    per_y = tops // ny
    assert per_y * half == nx and slab * 2 * nx == top_w and rows * 2 * nx == outer
    half_rows = top_w // 2
    part = half_rows // 2
    wide = num_rhs // nz
    chunk = wide // ny
    group = nz // half * chunk

    def vm(*shape, dtype=BF16):
        return pltpu.VMEM(shape, dtype)

    sems = pltpu.SemaphoreType.DMA
    results = pl.pallas_call(
        functools.partial(window_kernel, nz, nx, ny),
        out_shape=(
            jax.ShapeDtypeStruct(rhs_leaf.shape, BF16),
            jax.ShapeDtypeStruct(rhs_mid.shape, BF16),
            jax.ShapeDtypeStruct((per_y, slab, num_rhs), BF16),
            jax.ShapeDtypeStruct((chunk, rows), F32),
        ),
        in_specs=[smem] * 7 + [hbm] * 12,
        out_specs=(hbm,) * 4,
        scratch_shapes=[
            vm(leaves, leaf_w, num_rhs), vm(leaves, leaf_w, leaf_w), vm(leaves, mid_w, leaf_w),
            vm(mids, mid_w, num_rhs), vm(mids, mid_w, mid_w),
            vm(leaves, top_w, leaf_w), vm(mids, top_w, mid_w),
            vm(leaves, leaf_w, num_rhs), vm(mids, mid_w, num_rhs),
            vm(leaves, outer, leaf_w), vm(mids, outer, mid_w),
            vm(leaves * leaf_w + mids * mid_w, num_rhs),
            vm(mids, top_w, num_rhs), vm(mids, half_rows, num_rhs),
            vm(mids, max(tops, 8), LANES, dtype=F32), vm(mids, max(tops, 8), LANES, dtype=F32),
            vm(2, ny, nx, part, LANES),
            vm(nx - 1, ny, part, LANES), vm(ny - 1, nx, part, LANES),
            vm(ny, part, LANES), vm(nx, part, LANES),
            vm(ny - 1, part, LANES), vm(nx - 1, part, LANES),
            vm(2, half_rows, LANES), vm(nx, slab, top_w), vm(nx, slab, LANES),
            vm(nx, slab, LANES), vm(nx, slab, LANES), vm(per_y, slab, num_rhs),
            vm(ny, group, half_rows), vm(ny, nx, group, half_rows),
            vm(tops, 2, rows, half_rows),
            vm(2, nx, nz, wide, rows), vm(nx, nz, wide, rows), vm(nx, nz, wide, rows),
            vm(nz - 1, nx, wide, rows), vm(nx, wide, rows), vm(nx - 1, wide, rows),
            vm(ny, chunk, rows, dtype=F32), vm(ny - 1, chunk, rows, dtype=F32),
            vm(chunk, rows, dtype=F32),
            vm(2, nz, chunk, rows, dtype=F32), vm(2 * nz - 1, chunk, rows, dtype=F32),
            vm(chunk, rows, dtype=F32),
            sems((10,)), sems((4,)), sems((4 + mids,)), sems((4 + mids,)),
            sems((2, nx)), sems((2, nx)),
            sems((nx - 1,)), sems((nx - 1,)), sems((ny - 1,)), sems((ny - 1,)),
            sems((ny - 1,)), sems((ny - 1,)), sems((nx - 1,)), sems((nx - 1,)),
            sems((nx,)), sems((nx,)), sems((nx * ny - 1,)), sems((nx * ny - 1,)),
            sems((nz - 1,)), sems((nz - 1,)), sems((nx - 1,)), sems((nx - 1,)),
            sems((ny - 1,)), sems((ny - 1,)), sems((2 * nz - 1,)), sems((2 * nz - 1,)),
        ],
        compiler_params=pltpu.CompilerParams(
            collective_id=0, has_side_effects=True, vmem_limit_bytes=60 << 20
        ),
        name="window",
    )(
        parent_leaf.reshape(1, leaves), parent_mid.reshape(1, mids), width_leaf, width_mid,
        width_top, jnp.transpose(pattern_leaf[0], (1, 0)), pattern_mid,
        rhs_leaf, rhs_mid, rhs_top, inv_leaf, inv_mid, inv_top,
        off_leaf_mid, off_leaf_top, off_leaf_out, off_mid_top, off_mid_out, off_top_out,
    )
    leaf_x, mid_x, top_solution, outer_part = pl.pallas_call(
        finish_kernel,
        out_shape=tuple(jax.ShapeDtypeStruct(a.shape, a.dtype) for a in results),
        in_specs=[hbm] * 4,
        out_specs=(hbm,) * 4,
        scratch_shapes=[vm(*a.shape, dtype=a.dtype) for a in results] + [sems((4,)), sems((4,))],
        compiler_params=pltpu.CompilerParams(vmem_limit_bytes=60 << 20),
        name="finish",
    )(*results)
    return leaf_x, mid_x, top_solution, outer_part.T


def solution(mesh):
    sizes = dict(mesh.shape)
    deep = P("gz", ("pr", "pc"), None, None)
    flat = P("pr", "pc", None)
    return jax.shard_map(
        functools.partial(on_device, sizes["pr"], sizes["pc"] // 2, sizes["gz"]),
        mesh=mesh,
        in_specs=(
            deep, deep, flat, deep, deep, flat,
            deep, deep, deep, deep, deep, flat,
            P("gz", ("pr", "pc"), None),
            P("gz", ("pr", "pc"), None),
            P("gz", ("pr", "pc")),
            P("gz", ("pr", "pc")),
            P("pr"),
            P("gz", ("pr", "pc"), None),
            P("gz", ("pr", "pc")),
        ),
        out_specs=(deep, deep, P(("pr", "gz"), "pc", None), P("pc", ("pr", "gz"))),
        check_vma=False,
    )
```

```python
import functools

import jax
import jax.numpy as jnp
from jax import lax
from jax.experimental import pallas as pl
from jax.experimental.pallas import tpu as pltpu
from jax.sharding import PartitionSpec as P

MESH_IDS = pl.DeviceIdType.MESH
F32 = jnp.float32
BF16 = jnp.bfloat16
LANES = 128
CHUNKS = 2


def dot(a, b):
    return jnp.dot(a, b, preferred_element_type=F32)


def live_rows(values, first_row, width):
    row_ids = first_row + lax.broadcasted_iota(jnp.int32, values.shape, 0)
    return jnp.where(row_ids < width, values, 0.0)


def flagged(values, flag):
    return jnp.where(flag != 0, values, jnp.zeros_like(values))


def dot_nt(a, b):
    return lax.dot_general(a, b, (((1,), (1,)), ((), ())), preferred_element_type=F32)


def window_kernel(
    nz, nx, ny,
    parent_leaf_in, parent_mid_in, width_leaf_in, width_mid_in, width_top_in,
    pattern_leaf_in, pattern_mid_in,
    rhs_leaf, rhs_mid, rhs_top, inv_leaf, inv_mid, inv_top,
    off_leaf_mid, off_leaf_top, off_leaf_out, off_mid_top, off_mid_out, off_top_out,
    leaf_out, mid_out, top_solution, terms_out,
    parent_leaf, parent_mid, width_leaf, width_mid, width_top, pattern_leaf, pattern_mid,
    rl, il, lm, rm, im, lt, mt, xl, xm, ol, om, xo, xu, up_own, up_rx, mask, mask_rx,
    t_sum, a_rx, b_rx, a_sum, b_sum, a_rx2, b_rx2, top_in, inv, rhs,
    unit, sol_rx, sol_v, turned, gathered, wt,
    o_t, o_rx, o_s, o_rz, o_z, o_rx2, o_x, o_ry, q, own_v,
    vector_sems, load_sems, store_sems, core_s, core_r, pre_s, pre_r, a_s, a_r, b_s, b_r, a2_s, a2_r, b2_s, b2_r,
    sol_s, sol_r, g_s, g_r, oz_s, oz_r, ox_s, ox_r, oy_s, oy_r, q_s, q_r,
):
    z = lax.axis_index("pr")
    pc = lax.axis_index("pc")
    y = lax.axis_index("gz")
    x = pc // 2
    c = pc % 2
    other = 1 - c
    sibling = 2 * x + other
    leaves, mids = xl.shape[0], xm.shape[0]
    tops = rhs_top.shape[0]
    per_y = tops // ny
    half = xl.shape[2] // LANES
    slab = rhs_top.shape[1]
    chunks = t_sum.shape[0]
    part = t_sum.shape[4]
    block_rows = 2 * part
    half_rows = chunks * block_rows
    chunk = q.shape[2]
    rows = terms_out.shape[2]
    wide = o_t.shape[3]
    group = gathered.shape[2]
    num_rhs = xl.shape[2]

    def remote(src, dst, send, recv, device):
        return pltpu.make_async_remote_copy(
            src_ref=src, dst_ref=dst, send_sem=send, recv_sem=recv,
            device_id=device, device_id_type=MESH_IDS,
        )

    vectors = [
        pltpu.make_async_copy(src, dst, vector_sems.at[i]) for i, (src, dst) in enumerate((
            (width_leaf_in, width_leaf), (parent_leaf_in, parent_leaf), (parent_mid_in, parent_mid),
            (width_mid_in, width_mid), (pattern_leaf_in, pattern_leaf),
            (pattern_mid_in, pattern_mid), (width_top_in, width_top),
        ))
    ]
    load_pairs = [
        (inv_leaf.at[0], il), (rhs_leaf.at[0], rl), (off_leaf_mid.at[0], lm),
        (inv_mid.at[0], im), (rhs_mid.at[0], rm), (off_mid_top.at[0], mt), (off_leaf_top.at[0], lt),
        (off_leaf_out.at[0], ol), (off_mid_out.at[0], om),
        (off_top_out.at[:, :, pl.ds(pl.multiple_of(c * half_rows, half_rows), half_rows)], wt.at[:, c]),
    ]
    loads = [
        pltpu.make_async_copy(src, dst, load_sems.at[i]) for i, (src, dst) in enumerate(load_pairs)
    ]
    for load in loads[:2] + vectors + loads[2:7]:
        load.start()

    barrier = pltpu.get_barrier_semaphore()
    partners = [(z, lax.rem(pc + d, 2 * nx), y) for d in range(1, 2 * nx)]
    for dy in range(1, ny):
        for dx in range(nx):
            partners.append((z, lax.rem(pc + 2 * dx, 2 * nx), lax.rem(y + dy, ny)))
    for dz in range(1, nz):
        for core in range(2):
            partners.append((lax.rem(z + dz, nz), 2 * x + core, y))
    for partner in partners:
        pl.semaphore_signal(barrier, inc=1, device_id=partner, device_id_type=MESH_IDS)
    for vector in vectors:
        vector.wait()

    parents = [lax.rem(parent_leaf[0, k], mids) for k in range(leaves)]
    first, last = [], []
    for j in range(mids):
        low = jnp.int32(0)
        high = jnp.int32(0)
        for k in range(leaves):
            high = jnp.where(parents[k] == j, k, high)
            back = leaves - 1 - k
            low = jnp.where(parents[back] == j, back, low)
        first.append(low)
        last.append(high)
    for j in range(mids):
        ids = lax.broadcasted_iota(jnp.int32, mask.shape[1:], 0)
        mask[j] = jnp.where(ids == lax.rem(parent_mid[0, j], tops), 1.0, 0.0)

    loads[0].wait()
    loads[1].wait()
    for k in range(leaves):
        xl[k] = live_rows(dot(il[k], rl[k]), 0, width_leaf[0, k]).astype(BF16)
    store_leaf = pltpu.make_async_copy(xl, leaf_out.at[0], store_sems.at[0])
    store_leaf.start()

    for load in loads[2:5]:
        load.wait()
    for j in range(mids):
        total = dot(
            jnp.concatenate([lm[first[j]], lm[last[j]]], axis=1),
            jnp.concatenate([xl[first[j]], xl[last[j]]], axis=0),
        )
        mid_input = (rm[j].astype(F32) - total).astype(BF16)
        xm[j] = live_rows(dot(im[j], mid_input), 0, width_mid[0, j]).astype(BF16)
    store_mid = pltpu.make_async_copy(xm, mid_out.at[0], store_sems.at[1])
    store_mid.start()
    for load in loads[7:]:
        load.start()

    pl.semaphore_wait(barrier, len(partners))
    mask_copy = remote(mask, mask_rx, core_s.at[0], core_r.at[0], (z, sibling, y))
    mask_copy.start()

    slot = lax.rem(pc, nx)
    target_core = pc // nx
    pre_copies = []
    for d in range(nx):
        tx = lax.rem(x + d, nx)
        s = y * per_y + tx // half
        column = pl.multiple_of(lax.rem(tx, half) * LANES, LANES)
        pairs = (
            (inv_top.at[s], inv.at[slot]),
            (rhs_top.at[s, :, pl.ds(column, LANES)], rhs.at[slot]),
        )
        for i, (src, dst) in enumerate(pairs):
            copy = remote(
                src, dst, pre_s.at[i, d], pre_r.at[i, slot], (z, 2 * tx + target_core, y)
            )
            pre_copies.append((d, copy))
            if d == 0:
                @pl.when(target_core == c)
                def _():
                    pltpu.make_async_copy(src, dst, pre_r.at[i, slot]).start()

                @pl.when(target_core != c)
                def _():
                    copy.start()
            else:
                copy.start()

    loads[5].wait()
    loads[6].wait()
    for j in range(mids):
        low, high = first[j], last[j]
        xu[j] = jnp.concatenate([
            xm[j], flagged(xl[low], pattern_leaf[0, low]), flagged(xl[high], pattern_leaf[0, high])
        ], axis=0)
    up_copies = []
    for q_ in range(chunks):
        for j in range(mids):
            low, high = first[j], last[j]
            spans = [
                pl.ds(core * half_rows + q_ * block_rows, block_rows) for core in range(2)
            ]
            update = dot(
                jnp.concatenate([
                    jnp.concatenate([mt[j, span, :], lt[low, span, :], lt[high, span, :]], axis=1)
                    for span in spans
                ], axis=0),
                xu[j],
            )
            up_own[q_, j] = update.reshape(2, block_rows, num_rhs).astype(BF16)
            i = 1 + q_ * mids + j
            up_copies.append(remote(
                up_own.at[q_, j, other], up_rx.at[q_, j], core_s.at[i], core_r.at[i],
                (z, sibling, y),
            ))
            up_copies[-1].start()
    last_sem = 1 + chunks * mids
    w_copy = remote(
        off_top_out.at[:, :, pl.ds(pl.multiple_of(other * half_rows, half_rows), half_rows)],
        wt.at[:, c], core_s.at[last_sem], core_r.at[last_sem], (z, sibling, y),
    )

    mask_copy.wait_recv()
    step = 16
    far_x = sorted(range(1, nx), key=lambda d: -min(d, nx - d))
    far_y = sorted(range(1, ny), key=lambda d: -min(d, ny - d))
    a_copies, b_copies = [], []
    for q_ in range(chunks):
        for copy in up_copies[q_ * mids:(q_ + 1) * mids]:
            copy.wait_recv()
        for p in range(2):
            def pair_sum(i, carry):
                at = pl.multiple_of(i * step, step)
                span = pl.ds(pl.multiple_of(p * part + at, step), step)
                blocks = [up_own[q_, j, c, span, :].astype(F32) for j in range(mids)]
                blocks += [up_rx[q_, j, span, :].astype(F32) for j in range(mids)]
                for s in range(tops):
                    for h in range(half):
                        total = jnp.zeros((step, LANES), F32)
                        for j in range(2 * mids):
                            table = mask if j < mids else mask_rx
                            weight = table[j % mids, s:s + 1, :]
                            total += weight * blocks[j][:, h * LANES:(h + 1) * LANES]
                        t_sum[q_, p, s // per_y, (s % per_y) * half + h, pl.ds(at, step), :] = (
                            total.astype(BF16)
                        )
                return carry

            lax.fori_loop(0, part // step, pair_sum, 0)
            if p == 0:
                a_copies.append([])
                for d in far_x:
                    tx = lax.rem(x + d, nx)
                    a_copies[q_].append(remote(
                        t_sum.at[q_, 0, :, tx], a_rx.at[q_, d - 1],
                        a_s.at[q_, d - 1], a_r.at[q_, d - 1], (z, 2 * tx + c, y),
                    ))
                    a_copies[q_][-1].start()
            else:
                b_copies.append([])
                for d in far_y:
                    ty = lax.rem(y + d, ny)
                    b_copies[q_].append(remote(
                        t_sum.at[q_, 1, ty], b_rx.at[q_, d - 1],
                        b_s.at[q_, d - 1], b_r.at[q_, d - 1], (z, pc, ty),
                    ))
                    b_copies[q_][-1].start()
    w_copy.start()

    leaf_w, mid_w = xl.shape[1], xm.shape[1]
    for k in range(leaves):
        xo[k * leaf_w:(k + 1) * leaf_w] = flagged(xl[k], pattern_leaf[1, k])
    base = leaves * leaf_w
    for j in range(mids):
        xo[base + j * mid_w:base + (j + 1) * mid_w] = flagged(xm[j], pattern_mid[0, j])
    loads[7].wait()
    loads[8].wait()

    def outer_rows(i, carry):
        block = pl.ds(pl.multiple_of(i * 2 * rows, 2 * rows), 2 * rows)
        total = dot(
            jnp.concatenate(
                [ol[k, block, :] for k in range(leaves)] + [om[j, block, :] for j in range(mids)],
                axis=1,
            ),
            xo[...],
        )
        for core in range(2):
            across = total[core * rows:(core + 1) * rows].T
            o_t[core, i] = across.reshape(nz, wide, rows).astype(BF16)
        return carry

    lax.fori_loop(0, nx, outer_rows, 0)
    o_core = remote(
        o_t.at[other], o_rx, core_s.at[last_sem + 1], core_r.at[last_sem + 1], (z, sibling, y)
    )
    o_core.start()

    a2_copies, b2_copies = [], []
    for q_ in range(chunks):
        for copy in a_copies[q_]:
            copy.wait_recv()
        for i in range(ny):
            total = t_sum[q_, 0, i, x].astype(F32)
            for d in range(nx - 1):
                total += a_rx[q_, d, i].astype(F32)
            a_sum[q_, i] = total.astype(BF16)
        a2_copies.append([])
        for d in far_y:
            ty = lax.rem(y + d, ny)
            a2_copies[q_].append(remote(
                a_sum.at[q_, ty], a_rx2.at[q_, d - 1],
                a2_s.at[q_, d - 1], a2_r.at[q_, d - 1], (z, pc, ty),
            ))
            a2_copies[q_][-1].start()
        for copy in b_copies[q_]:
            copy.wait_recv()
        for i in range(nx):
            total = t_sum[q_, 1, y, i].astype(F32)
            for d in range(ny - 1):
                total += b_rx[q_, d, i].astype(F32)
            b_sum[q_, i] = total.astype(BF16)
        b2_copies.append([])
        for d in far_x:
            tx = lax.rem(x + d, nx)
            b2_copies[q_].append(remote(
                b_sum.at[q_, tx], b_rx2.at[q_, d - 1],
                b2_s.at[q_, d - 1], b2_r.at[q_, d - 1], (z, 2 * tx + c, y),
            ))
            b2_copies[q_][-1].start()
        if q_ == 0:
            o_core.wait_recv()
            oz_copies = []

            def outer_pair(i, carry):
                o_s[i] = (o_t[c, i].astype(F32) + o_rx[i].astype(F32)).astype(BF16)
                return carry

            lax.fori_loop(0, nx, outer_pair, 0)
            for d in range(1, nz):
                tz = lax.rem(z + d, nz)
                oz_copies.append(remote(
                    o_s.at[:, tz], o_rz.at[d - 1], oz_s.at[d - 1], oz_r.at[d - 1], (tz, pc, y),
                ))
                oz_copies[-1].start()

    for i in range(nx):
        pre = [
            remote(inv_top.at[0], inv.at[i], pre_s.at[0, 0], pre_r.at[0, i], (z, sibling, y)),
            remote(rhs_top.at[0, :, pl.ds(0, LANES)], rhs.at[i], pre_s.at[1, 0], pre_r.at[1, i],
                   (z, sibling, y)),
        ]
        for copy in pre:
            copy.wait_recv()
    right = rhs[...].reshape(chunks, 2, part, LANES).astype(F32)
    in_copies = []
    for q_ in range(chunks):
        for copy in a2_copies[q_]:
            copy.wait_recv()
        total = a_sum[q_, y].astype(F32)
        for d in range(ny - 1):
            total += a_rx2[q_, d].astype(F32)
        top_in[c, q_, pl.ds(0, part), :] = (right[q_, 0] - total).astype(BF16)
        for copy in b2_copies[q_]:
            copy.wait_recv()
        total = b_sum[q_, x].astype(F32)
        for d in range(nx - 1):
            total += b_rx2[q_, d].astype(F32)
        top_in[c, q_, pl.ds(part, part), :] = (right[q_, 1] - total).astype(BF16)
        i = last_sem + 2 + q_
        in_copies.append(remote(
            top_in.at[c, q_], top_in.at[c, q_], core_s.at[i], core_r.at[i], (z, sibling, y)
        ))
        in_copies[-1].start()
    for copy in in_copies:
        copy.wait_recv()

    block = dot(inv[...].reshape(half_rows, inv.shape[2]), top_in[...].reshape(2 * half_rows, LANES))
    block = live_rows(block, c * half_rows, width_top[y * per_y + x // half])
    across = block.T.reshape(nz // half, ny, chunk, half_rows)
    for i in range(ny):
        turned[i] = across[:, i].reshape(group, half_rows).astype(BF16)
    unit[...] = block.reshape(nx, slab, LANES).astype(BF16)

    g_copies = []
    steps = [(dx, dy) for dy in range(ny) for dx in range(nx) if dx or dy]
    for dx, dy in sorted(steps, key=lambda d: -min(d[0], nx - d[0]) - min(d[1], ny - d[1])):
        tx = lax.rem(x + dx, nx)
        ty = lax.rem(y + dy, ny)
        i = dy * nx + dx - 1
        g_copies.append(remote(
            turned.at[ty], gathered.at[y, x], g_s.at[i], g_r.at[i], (z, 2 * tx + c, ty),
        ))
        g_copies[-1].start()
    gathered[y, x] = turned[y]

    sol_copies = []
    for d in range(nx):
        i = lax.rem(slot + d, nx)
        copy = remote(
            unit.at[i], sol_rx.at[x], sol_s.at[d], sol_r.at[x], (z, nx * c + i, y)
        )
        sol_copies.append((d, copy))
        if d == 0:
            @pl.when(target_core == c)
            def _():
                pltpu.make_async_copy(unit.at[i], sol_rx.at[x], sol_r.at[x]).start()

            @pl.when(target_core != c)
            def _():
                copy.start()
        else:
            copy.start()

    for copy in oz_copies:
        copy.wait_recv()
    ox_copies = []
    for i in range(nx):
        total = o_s[i, z].astype(F32)
        for d in range(nz - 1):
            total += o_rz[d, i].astype(F32)
        o_z[i] = total.astype(BF16)
    for d in range(1, nx):
        tx = lax.rem(x + d, nx)
        ox_copies.append(remote(
            o_z.at[tx], o_rx2.at[d - 1], ox_s.at[d - 1], ox_r.at[d - 1], (z, 2 * tx + c, y),
        ))
        ox_copies[-1].start()

    loads[9].wait()
    w_copy.wait_recv()
    for copy in g_copies:
        copy.wait_recv()

    total = jnp.zeros((half * group, 2 * rows), F32)
    for i in range(ny):
        for t in range(per_y):
            left = gathered[i, t * half:(t + 1) * half].reshape(half * group, half_rows)
            total += dot_nt(left, wt[i * per_y + t].reshape(2 * rows, half_rows))
    for core in range(2):
        q[core] = total[:, core * rows:(core + 1) * rows].reshape(nz, chunk, rows)
    q_copies = []
    steps = [(dz, dc) for dz in range(nz) for dc in range(2) if dz or dc]
    for dz, dc in sorted(steps, key=lambda d: -min(d[0], nz - d[0])):
        tz = lax.rem(z + dz, nz)
        tc = lax.rem(c + dc, 2)
        i = 2 * dz + dc - 1
        q_copies.append(remote(
            q.at[tc, tz], terms_out.at[i], q_s.at[i], q_r.at[i], (tz, 2 * x + tc, y),
        ))
        q_copies[-1].start()

    for copy in ox_copies:
        copy.wait_recv()
    total = o_z[x].astype(F32)
    for d in range(nx - 1):
        total += o_rx2[d].astype(F32)
    o_x[...] = total.reshape(ny, chunk, rows)
    oy_copies = []
    for d in range(1, ny):
        ty = lax.rem(y + d, ny)
        oy_copies.append(remote(
            o_x.at[ty], o_ry.at[d - 1], oy_s.at[d - 1], oy_r.at[d - 1], (z, pc, ty),
        ))
        oy_copies[-1].start()
    for i in range(nx):
        remote(unit.at[0], sol_rx.at[i], sol_s.at[0], sol_r.at[i], (z, sibling, y)).wait_recv()
    for t in range(per_y):
        for h in range(half):
            sol_v[t, :, h * LANES:(h + 1) * LANES] = sol_rx[t * half + h]
    store_sol = pltpu.make_async_copy(sol_v, top_solution, store_sems.at[2])
    store_sol.start()
    for copy in oy_copies:
        copy.wait_recv()
    total = o_x[y]
    for d in range(ny - 1):
        total += o_ry[d]
    own_v[...] = total + q[c, z]
    store_own = pltpu.make_async_copy(own_v, terms_out.at[2 * nz - 1], store_sems.at[3])
    store_own.start()

    for copy in (
        [mask_copy, w_copy, o_core] + in_copies + up_copies
        + sum(a_copies + b_copies + a2_copies + b2_copies, [])
        + g_copies + oz_copies + ox_copies + oy_copies
    ):
        copy.wait_send()
    for d, copy in pre_copies + sol_copies:
        if d == 0:
            @pl.when(target_core != c)
            def _():
                copy.wait_send()
        else:
            copy.wait_send()
    store_leaf.wait()
    store_mid.wait()
    store_sol.wait()
    store_own.wait()
    for copy in q_copies:
        copy.wait_recv()
    for copy in q_copies:
        copy.wait_send()


def finish_kernel(*refs):
    count = (len(refs) - 3) // 3
    ins, outs, held = refs[:count], refs[count:2 * count], refs[2 * count:3 * count]
    outer_v, in_sems, out_sems = refs[-3:]
    loads = [pltpu.make_async_copy(ins[i], held[i], in_sems.at[i]) for i in range(count)]
    for load in loads:
        load.start()
    stores = []
    for i in range(count):
        loads[i].wait()
        if i == count - 1:
            total = held[i][0]
            for d in range(1, held[i].shape[0]):
                total += held[i][d]
            outer_v[...] = total
        source = outer_v if i == count - 1 else held[i]
        stores.append(pltpu.make_async_copy(source, outs[i], out_sems.at[i]))
        stores[-1].start()
    for store in stores:
        store.wait()


def on_device(
    nz, nx, ny,
    rhs_leaf, rhs_mid, rhs_top, inv_leaf, inv_mid, inv_top,
    off_leaf_mid, off_leaf_top, off_leaf_out, off_mid_top, off_mid_out, off_top_out,
    parent_leaf, parent_mid, width_leaf, width_mid, width_top, pattern_leaf, pattern_mid,
):
    hbm = pl.BlockSpec(memory_space=pl.ANY)
    leaves, leaf_w, num_rhs = rhs_leaf.shape[1:]
    mids, mid_w = rhs_mid.shape[1:3]
    tops, slab = rhs_top.shape[:2]
    top_w = inv_top.shape[2]
    outer = off_leaf_out.shape[2]
    rows = off_top_out.shape[1]
    half = num_rhs // LANES
    per_y = tops // ny
    assert per_y * half == nx and slab * 2 * nx == top_w and rows * 2 * nx == outer
    half_rows = top_w // 2
    chunks = CHUNKS
    part = half_rows // chunks // 2
    wide = num_rhs // nz
    chunk = wide // ny
    group = nz // half * chunk

    def vm(*shape, dtype=BF16):
        return pltpu.VMEM(shape, dtype)

    sems = pltpu.SemaphoreType.DMA
    results = pl.pallas_call(
        functools.partial(window_kernel, nz, nx, ny),
        out_shape=(
            jax.ShapeDtypeStruct(rhs_leaf.shape, BF16),
            jax.ShapeDtypeStruct(rhs_mid.shape, BF16),
            jax.ShapeDtypeStruct((per_y, slab, num_rhs), BF16),
            jax.ShapeDtypeStruct((2 * nz, chunk, rows), F32),
        ),
        in_specs=[hbm] * 19,
        out_specs=(hbm,) * 4,
        scratch_shapes=[
            pltpu.SMEM((1, leaves), jnp.int32), pltpu.SMEM((1, mids), jnp.int32),
            pltpu.SMEM((1, leaves), jnp.int32), pltpu.SMEM((1, mids), jnp.int32),
            pltpu.SMEM((tops,), jnp.int32), pltpu.SMEM((2, leaves), jnp.int32),
            pltpu.SMEM((1, mids), jnp.int32),
            vm(leaves, leaf_w, num_rhs), vm(leaves, leaf_w, leaf_w), vm(leaves, mid_w, leaf_w),
            vm(mids, mid_w, num_rhs), vm(mids, mid_w, mid_w),
            vm(leaves, top_w, leaf_w), vm(mids, top_w, mid_w),
            vm(leaves, leaf_w, num_rhs), vm(mids, mid_w, num_rhs),
            vm(leaves, outer, leaf_w), vm(mids, outer, mid_w),
            vm(leaves * leaf_w + mids * mid_w, num_rhs),
            vm(mids, mid_w + 2 * leaf_w, num_rhs),
            vm(chunks, mids, 2, 2 * part, num_rhs), vm(chunks, mids, 2 * part, num_rhs),
            vm(mids, max(tops, 8), LANES, dtype=F32), vm(mids, max(tops, 8), LANES, dtype=F32),
            vm(chunks, 2, ny, nx, part, LANES),
            vm(chunks, nx - 1, ny, part, LANES), vm(chunks, ny - 1, nx, part, LANES),
            vm(chunks, ny, part, LANES), vm(chunks, nx, part, LANES),
            vm(chunks, ny - 1, part, LANES), vm(chunks, nx - 1, part, LANES),
            vm(2, chunks, 2 * part, LANES), vm(nx, slab, top_w), vm(nx, slab, LANES),
            vm(nx, slab, LANES), vm(nx, slab, LANES), vm(per_y, slab, num_rhs),
            vm(ny, group, half_rows), vm(ny, nx, group, half_rows),
            vm(tops, 2, rows, half_rows),
            vm(2, nx, nz, wide, rows), vm(nx, nz, wide, rows), vm(nx, nz, wide, rows),
            vm(nz - 1, nx, wide, rows), vm(nx, wide, rows), vm(nx - 1, wide, rows),
            vm(ny, chunk, rows, dtype=F32), vm(ny - 1, chunk, rows, dtype=F32),
            vm(2, nz, chunk, rows, dtype=F32), vm(chunk, rows, dtype=F32),
            sems((7,)), sems((10,)), sems((4,)),
            sems((3 + chunks * (mids + 1),)), sems((3 + chunks * (mids + 1),)),
            sems((2, nx)), sems((2, nx)),
            sems((chunks, nx - 1)), sems((chunks, nx - 1)),
            sems((chunks, ny - 1)), sems((chunks, ny - 1)),
            sems((chunks, ny - 1)), sems((chunks, ny - 1)),
            sems((chunks, nx - 1)), sems((chunks, nx - 1)),
            sems((nx,)), sems((nx,)), sems((nx * ny - 1,)), sems((nx * ny - 1,)),
            sems((nz - 1,)), sems((nz - 1,)), sems((nx - 1,)), sems((nx - 1,)),
            sems((ny - 1,)), sems((ny - 1,)), sems((2 * nz - 1,)), sems((2 * nz - 1,)),
        ],
        compiler_params=pltpu.CompilerParams(
            collective_id=0, has_side_effects=True, vmem_limit_bytes=60 << 20
        ),
        name="window",
    )(
        parent_leaf.reshape(1, leaves), parent_mid.reshape(1, mids), width_leaf, width_mid,
        width_top, jnp.transpose(pattern_leaf[0], (1, 0)), pattern_mid,
        rhs_leaf, rhs_mid, rhs_top, inv_leaf, inv_mid, inv_top,
        off_leaf_mid, off_leaf_top, off_leaf_out, off_mid_top, off_mid_out, off_top_out,
    )
    shapes = [jax.ShapeDtypeStruct(a.shape, a.dtype) for a in results[:3]]
    shapes.append(jax.ShapeDtypeStruct((chunk, rows), F32))
    leaf_x, mid_x, top_solution, outer_part = pl.pallas_call(
        finish_kernel,
        out_shape=tuple(shapes),
        in_specs=[hbm] * 4,
        out_specs=(hbm,) * 4,
        scratch_shapes=[vm(*a.shape, dtype=a.dtype) for a in results]
        + [vm(chunk, rows, dtype=F32), sems((4,)), sems((4,))],
        compiler_params=pltpu.CompilerParams(vmem_limit_bytes=60 << 20),
        name="finish",
    )(*results)
    return leaf_x, mid_x, top_solution, outer_part.T


def solution(mesh):
    sizes = dict(mesh.shape)
    deep = P("gz", ("pr", "pc"), None, None)
    flat = P("pr", "pc", None)
    return jax.shard_map(
        functools.partial(on_device, sizes["pr"], sizes["pc"] // 2, sizes["gz"]),
        mesh=mesh,
        in_specs=(
            deep, deep, flat, deep, deep, flat,
            deep, deep, deep, deep, deep, flat,
            P("gz", ("pr", "pc"), None),
            P("gz", ("pr", "pc"), None),
            P("gz", ("pr", "pc")),
            P("gz", ("pr", "pc")),
            P("pr"),
            P("gz", ("pr", "pc"), None),
            P("gz", ("pr", "pc")),
        ),
        out_specs=(deep, deep, P(("pr", "gz"), "pc", None), P("pc", ("pr", "gz"))),
        check_vma=False,
    )
```

```python
import functools

import jax
import jax.numpy as jnp
from jax import lax
from jax.experimental import pallas as pl
from jax.experimental.pallas import tpu as pltpu
from jax.sharding import PartitionSpec as P

MESH_IDS = pl.DeviceIdType.MESH
F32 = jnp.float32
BF16 = jnp.bfloat16
LANES = 128
CHUNKS = 2


def dot(a, b):
    return jnp.dot(a, b, preferred_element_type=F32)


def live_rows(values, first_row, width):
    row_ids = first_row + lax.broadcasted_iota(jnp.int32, values.shape, 0)
    return jnp.where(row_ids < width, values, 0.0)


def flagged(values, flag):
    return jnp.where(flag != 0, values, jnp.zeros_like(values))


def dot_nt(a, b):
    return lax.dot_general(a, b, (((1,), (1,)), ((), ())), preferred_element_type=F32)


def window_kernel(
    nz, nx, ny,
    parent_leaf_in, parent_mid_in, width_leaf_in, width_mid_in, width_top_in,
    pattern_leaf_in, pattern_mid_in,
    rhs_leaf, rhs_mid, rhs_top, inv_leaf, inv_mid, inv_top,
    off_leaf_mid, off_leaf_top, off_leaf_out, off_mid_top, off_mid_out, off_top_out,
    leaf_out, mid_out, top_solution, terms_out,
    parent_leaf, parent_mid, width_leaf, width_mid, width_top, pattern_leaf, pattern_mid,
    rl, il, lm, rm, im, lt, mt, ol, om, xo, xu, up_own, up_rx, mask, mask_rx,
    t_sum, a_rx, b_rx, a_sum, b_sum, a_rx2, b_rx2, top_in, inv, rhs,
    unit, sol_rx, turned, gathered, wt,
    o_t, o_rx, o_s, o_rz, o_z, o_rx2, o_x, o_ry, q,
    vector_sems, load_sems, core_s, core_r, pre_s, pre_r, a_s, a_r, b_s, b_r, a2_s, a2_r, b2_s, b2_r,
    sol_s, sol_r, g_s, g_r, oz_s, oz_r, ox_s, ox_r, oy_s, oy_r, q_s, q_r,
):
    z = lax.axis_index("pr")
    pc = lax.axis_index("pc")
    y = lax.axis_index("gz")
    x = pc // 2
    c = pc % 2
    other = 1 - c
    sibling = 2 * x + other
    xl, xm = leaf_out.at[0], mid_out.at[0]
    leaves, mids = xl.shape[0], xm.shape[0]
    tops = rhs_top.shape[0]
    per_y = tops // ny
    half = xl.shape[2] // LANES
    slab = rhs_top.shape[1]
    chunks = t_sum.shape[0]
    part = t_sum.shape[4]
    block_rows = 2 * part
    half_rows = chunks * block_rows
    chunk = q.shape[2]
    rows = terms_out.shape[2]
    wide = o_t.shape[3]
    group = gathered.shape[2]
    num_rhs = xl.shape[2]

    def remote(src, dst, send, recv, device):
        return pltpu.make_async_remote_copy(
            src_ref=src, dst_ref=dst, send_sem=send, recv_sem=recv,
            device_id=device, device_id_type=MESH_IDS,
        )

    vectors = [
        pltpu.make_async_copy(src, dst, vector_sems.at[i]) for i, (src, dst) in enumerate((
            (width_leaf_in, width_leaf), (parent_leaf_in, parent_leaf), (parent_mid_in, parent_mid),
            (width_mid_in, width_mid), (pattern_leaf_in, pattern_leaf),
            (pattern_mid_in, pattern_mid), (width_top_in, width_top),
        ))
    ]
    load_pairs = [
        (inv_leaf.at[0], il), (rhs_leaf.at[0], rl), (off_leaf_mid.at[0], lm),
        (inv_mid.at[0], im), (rhs_mid.at[0], rm), (off_mid_top.at[0], mt), (off_leaf_top.at[0], lt),
        (off_leaf_out.at[0], ol), (off_mid_out.at[0], om),
        (off_top_out.at[:, :, pl.ds(pl.multiple_of(c * half_rows, half_rows), half_rows)], wt.at[:, c]),
    ]
    loads = [
        pltpu.make_async_copy(src, dst, load_sems.at[i]) for i, (src, dst) in enumerate(load_pairs)
    ]
    for load in loads[:2] + vectors[:4] + loads[2:5]:
        load.start()

    barrier = pltpu.get_barrier_semaphore()
    partners = []
    for d in sorted(range(1, nz), key=lambda d: -min(d, nz - d)):
        for core in range(2):
            partners.append((lax.rem(z + d, nz), 2 * x + core, y))
    steps = [(dx, dy) for dy in range(ny) for dx in range(nx) if dx or dy]
    for dx, dy in sorted(steps, key=lambda d: -min(d[0], nx - d[0]) - min(d[1], ny - d[1])):
        partners.append((z, 2 * lax.rem(x + dx, nx) + c, lax.rem(y + dy, ny)))
    for dx in range(nx):
        partners.append((z, 2 * lax.rem(x + dx, nx) + other, y))
    for partner in partners:
        pl.semaphore_signal(barrier, inc=1, device_id=partner, device_id_type=MESH_IDS)
    for load in loads[5:7] + vectors[4:]:
        load.start()
    for vector in vectors:
        vector.wait()

    parents = [lax.rem(parent_leaf[0, k], mids) for k in range(leaves)]
    first, last = [], []
    for j in range(mids):
        low = jnp.int32(0)
        high = jnp.int32(0)
        for k in range(leaves):
            high = jnp.where(parents[k] == j, k, high)
            back = leaves - 1 - k
            low = jnp.where(parents[back] == j, back, low)
        first.append(low)
        last.append(high)
    for j in range(mids):
        ids = lax.broadcasted_iota(jnp.int32, mask.shape[1:], 0)
        mask[j] = jnp.where(ids == lax.rem(parent_mid[0, j], tops), 1.0, 0.0)

    loads[0].wait()
    loads[1].wait()
    for k in range(leaves):
        xl[k] = live_rows(dot(il[k], rl[k]), 0, width_leaf[0, k]).astype(BF16)

    for load in loads[2:5]:
        load.wait()
    for j in range(mids):
        total = dot(
            jnp.concatenate([lm[first[j]], lm[last[j]]], axis=1),
            jnp.concatenate([xl[first[j]], xl[last[j]]], axis=0),
        )
        mid_input = (rm[j].astype(F32) - total).astype(BF16)
        xm[j] = live_rows(dot(im[j], mid_input), 0, width_mid[0, j]).astype(BF16)
    for load in loads[7:]:
        load.start()

    loads[5].wait()
    loads[6].wait()
    for j in range(mids):
        low, high = first[j], last[j]
        xu[j] = jnp.concatenate([
            xm[j], flagged(xl[low], pattern_leaf[0, low]), flagged(xl[high], pattern_leaf[0, high])
        ], axis=0)
    up_copies = []
    for q_ in range(chunks):
        for j in range(mids):
            low, high = first[j], last[j]
            spans = [
                pl.ds(core * half_rows + q_ * block_rows, block_rows) for core in range(2)
            ]
            update = dot(
                jnp.concatenate([
                    jnp.concatenate([mt[j, span, :], lt[low, span, :], lt[high, span, :]], axis=1)
                    for span in spans
                ], axis=0),
                xu[j],
            )
            for core in range(2):
                up_own[q_, core, j] = update[core * block_rows:(core + 1) * block_rows].astype(BF16)
        if q_ == 0:
            pl.semaphore_wait(barrier, len(partners))
            mask_copy = remote(mask, mask_rx, core_s.at[0], core_r.at[0], (z, sibling, y))
            mask_copy.start()
        up_copies.append(remote(
            up_own.at[q_, other], up_rx.at[q_], core_s.at[1 + q_], core_r.at[1 + q_], (z, sibling, y)
        ))
        up_copies[-1].start()
    last_sem = 1 + chunks
    w_copy = remote(
        off_top_out.at[:, :, pl.ds(pl.multiple_of(other * half_rows, half_rows), half_rows)],
        wt.at[:, c], core_s.at[last_sem], core_r.at[last_sem], (z, sibling, y),
    )

    mask_copy.wait_recv()
    step = 16
    far_x = sorted(range(1, nx), key=lambda d: -min(d, nx - d))
    far_y = sorted(range(1, ny), key=lambda d: -min(d, ny - d))
    a_copies, b_copies = [], []
    for q_ in range(chunks):
        up_copies[q_].wait_recv()
        for p in range(2):
            def pair_sum(i, carry):
                at = pl.multiple_of(i * step, step)
                span = pl.ds(pl.multiple_of(p * part + at, step), step)
                blocks = [up_own[q_, c, j, span, :].astype(F32) for j in range(mids)]
                blocks += [up_rx[q_, j, span, :].astype(F32) for j in range(mids)]
                for s in range(tops):
                    for h in range(half):
                        total = jnp.zeros((step, LANES), F32)
                        for j in range(2 * mids):
                            table = mask if j < mids else mask_rx
                            weight = table[j % mids, s:s + 1, :]
                            total += weight * blocks[j][:, h * LANES:(h + 1) * LANES]
                        t_sum[q_, p, s // per_y, (s % per_y) * half + h, pl.ds(at, step), :] = (
                            total.astype(BF16)
                        )
                return carry

            lax.fori_loop(0, part // step, pair_sum, 0)
            if p == 0:
                a_copies.append([])
                for d in far_x:
                    tx = lax.rem(x + d, nx)
                    a_copies[q_].append(remote(
                        t_sum.at[q_, 0, :, tx], a_rx.at[q_, d - 1],
                        a_s.at[q_, d - 1], a_r.at[q_, d - 1], (z, 2 * tx + c, y),
                    ))
                    a_copies[q_][-1].start()
            else:
                b_copies.append([])
                for d in far_y:
                    ty = lax.rem(y + d, ny)
                    b_copies[q_].append(remote(
                        t_sum.at[q_, 1, ty], b_rx.at[q_, d - 1],
                        b_s.at[q_, d - 1], b_r.at[q_, d - 1], (z, pc, ty),
                    ))
                    b_copies[q_][-1].start()
    slot = lax.rem(pc, nx)
    target_core = pc // nx
    pre_copies = []
    for d in range(nx):
        tx = lax.rem(x + d, nx)
        s = y * per_y + tx // half
        column = pl.multiple_of(lax.rem(tx, half) * LANES, LANES)
        pairs = (
            (inv_top.at[s], inv.at[slot]),
            (rhs_top.at[s, :, pl.ds(column, LANES)], rhs.at[slot]),
        )
        for i, (src, dst) in enumerate(pairs):
            copy = remote(
                src, dst, pre_s.at[i, d], pre_r.at[i, slot], (z, 2 * tx + target_core, y)
            )
            pre_copies.append((d, copy))
            if d == 0:
                @pl.when(target_core == c)
                def _():
                    pltpu.make_async_copy(src, dst, pre_r.at[i, slot]).start()

                @pl.when(target_core != c)
                def _():
                    copy.start()
            else:
                copy.start()

    w_copy.start()

    leaf_w, mid_w = xl.shape[1], xm.shape[1]
    for k in range(leaves):
        xo[k * leaf_w:(k + 1) * leaf_w] = flagged(xl[k], pattern_leaf[1, k])
    base = leaves * leaf_w
    for j in range(mids):
        xo[base + j * mid_w:base + (j + 1) * mid_w] = flagged(xm[j], pattern_mid[0, j])
    loads[7].wait()
    loads[8].wait()

    def outer_rows(i, carry):
        block = pl.ds(pl.multiple_of(i * 2 * rows, 2 * rows), 2 * rows)
        total = dot(
            jnp.concatenate(
                [ol[k, block, :] for k in range(leaves)] + [om[j, block, :] for j in range(mids)],
                axis=1,
            ),
            xo[...],
        )
        for core in range(2):
            across = total[core * rows:(core + 1) * rows].T
            o_t[core, i] = across.reshape(nz, wide, rows).astype(BF16)
        return carry

    lax.fori_loop(0, nx, outer_rows, 0)
    o_core = remote(
        o_t.at[other], o_rx, core_s.at[last_sem + 1], core_r.at[last_sem + 1], (z, sibling, y)
    )
    o_core.start()

    a2_copies, b2_copies = [], []
    for q_ in range(chunks):
        for copy in a_copies[q_]:
            copy.wait_recv()
        for i in range(ny):
            total = t_sum[q_, 0, i, x].astype(F32)
            for d in range(nx - 1):
                total += a_rx[q_, d, i].astype(F32)
            a_sum[q_, i] = total.astype(BF16)
        a2_copies.append([])
        for d in far_y:
            ty = lax.rem(y + d, ny)
            a2_copies[q_].append(remote(
                a_sum.at[q_, ty], a_rx2.at[q_, d - 1],
                a2_s.at[q_, d - 1], a2_r.at[q_, d - 1], (z, pc, ty),
            ))
            a2_copies[q_][-1].start()
        for copy in b_copies[q_]:
            copy.wait_recv()
        for i in range(nx):
            total = t_sum[q_, 1, y, i].astype(F32)
            for d in range(ny - 1):
                total += b_rx[q_, d, i].astype(F32)
            b_sum[q_, i] = total.astype(BF16)
        b2_copies.append([])
        for d in far_x:
            tx = lax.rem(x + d, nx)
            b2_copies[q_].append(remote(
                b_sum.at[q_, tx], b_rx2.at[q_, d - 1],
                b2_s.at[q_, d - 1], b2_r.at[q_, d - 1], (z, 2 * tx + c, y),
            ))
            b2_copies[q_][-1].start()
        if q_ == 0:
            o_core.wait_recv()
            oz_copies = []

            def outer_pair(i, carry):
                o_s[i] = (o_t[c, i].astype(F32) + o_rx[i].astype(F32)).astype(BF16)
                return carry

            lax.fori_loop(0, nx, outer_pair, 0)
            for d in range(1, nz):
                tz = lax.rem(z + d, nz)
                oz_copies.append(remote(
                    o_s.at[:, tz], o_rz.at[d - 1], oz_s.at[d - 1], oz_r.at[d - 1], (tz, pc, y),
                ))
                oz_copies[-1].start()

    for i in range(nx):
        pre = [
            remote(inv_top.at[0], inv.at[i], pre_s.at[0, 0], pre_r.at[0, i], (z, sibling, y)),
            remote(rhs_top.at[0, :, pl.ds(0, LANES)], rhs.at[i], pre_s.at[1, 0], pre_r.at[1, i],
                   (z, sibling, y)),
        ]
        for copy in pre:
            copy.wait_recv()
    right = rhs[...].reshape(chunks, 2, part, LANES).astype(F32)
    in_copies = []
    for q_ in range(chunks):
        for copy in a2_copies[q_]:
            copy.wait_recv()
        total = a_sum[q_, y].astype(F32)
        for d in range(ny - 1):
            total += a_rx2[q_, d].astype(F32)
        top_in[c, q_, pl.ds(0, part), :] = (right[q_, 0] - total).astype(BF16)
        for copy in b2_copies[q_]:
            copy.wait_recv()
        total = b_sum[q_, x].astype(F32)
        for d in range(nx - 1):
            total += b_rx2[q_, d].astype(F32)
        top_in[c, q_, pl.ds(part, part), :] = (right[q_, 1] - total).astype(BF16)
        i = last_sem + 2 + q_
        in_copies.append(remote(
            top_in.at[c, q_], top_in.at[c, q_], core_s.at[i], core_r.at[i], (z, sibling, y)
        ))
        in_copies[-1].start()
    for copy in in_copies:
        copy.wait_recv()

    block = dot(inv[...].reshape(half_rows, inv.shape[2]), top_in[...].reshape(2 * half_rows, LANES))
    block = live_rows(block, c * half_rows, width_top[y * per_y + x // half])
    across = block.T.reshape(nz // half, ny, chunk, half_rows)
    for i in range(ny):
        turned[i] = across[:, i].reshape(group, half_rows).astype(BF16)
    unit[...] = block.reshape(nx, slab, LANES).astype(BF16)

    g_copies = []
    steps = [(dx, dy) for dy in range(ny) for dx in range(nx) if dx or dy]
    for dx, dy in sorted(steps, key=lambda d: -min(d[0], nx - d[0]) - min(d[1], ny - d[1])):
        tx = lax.rem(x + dx, nx)
        ty = lax.rem(y + dy, ny)
        i = dy * nx + dx - 1
        g_copies.append(remote(
            turned.at[ty], gathered.at[y, x], g_s.at[i], g_r.at[i], (z, 2 * tx + c, ty),
        ))
        g_copies[-1].start()
    gathered[y, x] = turned[y]

    sol_copies = []
    for d in range(nx):
        i = lax.rem(slot + d, nx)
        copy = remote(
            unit.at[i], sol_rx.at[x], sol_s.at[d], sol_r.at[x], (z, nx * c + i, y)
        )
        sol_copies.append((d, copy))
        if d == 0:
            @pl.when(target_core == c)
            def _():
                pltpu.make_async_copy(unit.at[i], sol_rx.at[x], sol_r.at[x]).start()

            @pl.when(target_core != c)
            def _():
                copy.start()
        else:
            copy.start()

    for copy in oz_copies:
        copy.wait_recv()
    ox_copies = []
    for i in range(nx):
        total = o_s[i, z].astype(F32)
        for d in range(nz - 1):
            total += o_rz[d, i].astype(F32)
        o_z[i] = total.astype(BF16)
    for d in range(1, nx):
        tx = lax.rem(x + d, nx)
        ox_copies.append(remote(
            o_z.at[tx], o_rx2.at[d - 1], ox_s.at[d - 1], ox_r.at[d - 1], (z, 2 * tx + c, y),
        ))
        ox_copies[-1].start()

    loads[9].wait()
    w_copy.wait_recv()
    for copy in g_copies:
        copy.wait_recv()

    total = jnp.zeros((half * group, 2 * rows), F32)
    for i in range(ny):
        for t in range(per_y):
            left = gathered[i, t * half:(t + 1) * half].reshape(half * group, half_rows)
            total += dot_nt(left, wt[i * per_y + t].reshape(2 * rows, half_rows))
    for core in range(2):
        q[core] = total[:, core * rows:(core + 1) * rows].reshape(nz, chunk, rows)
    q_copies = []
    steps = [(dz, dc) for dz in range(nz) for dc in range(2) if dz or dc]
    for dz, dc in sorted(steps, key=lambda d: -min(d[0], nz - d[0])):
        tz = lax.rem(z + dz, nz)
        tc = lax.rem(c + dc, 2)
        i = 2 * dz + dc - 1
        q_copies.append(remote(
            q.at[tc, tz], terms_out.at[i], q_s.at[i], q_r.at[i], (tz, 2 * x + tc, y),
        ))
        q_copies[-1].start()

    for copy in ox_copies:
        copy.wait_recv()
    total = o_z[x].astype(F32)
    for d in range(nx - 1):
        total += o_rx2[d].astype(F32)
    o_x[...] = total.reshape(ny, chunk, rows)
    oy_copies = []
    for d in range(1, ny):
        ty = lax.rem(y + d, ny)
        oy_copies.append(remote(
            o_x.at[ty], o_ry.at[d - 1], oy_s.at[d - 1], oy_r.at[d - 1], (z, pc, ty),
        ))
        oy_copies[-1].start()
    for i in range(nx):
        remote(unit.at[0], sol_rx.at[i], sol_s.at[0], sol_r.at[i], (z, sibling, y)).wait_recv()
    for t in range(per_y):
        for h in range(half):
            top_solution[t, :, h * LANES:(h + 1) * LANES] = sol_rx[t * half + h]
    for copy in oy_copies:
        copy.wait_recv()
    total = o_x[y]
    for d in range(ny - 1):
        total += o_ry[d]
    terms_out[2 * nz - 1] = total + q[c, z]

    for copy in (
        [mask_copy, w_copy, o_core] + in_copies + up_copies
        + sum(a_copies + b_copies + a2_copies + b2_copies, [])
        + g_copies + oz_copies + ox_copies + oy_copies
    ):
        copy.wait_send()
    for d, copy in pre_copies + sol_copies:
        if d == 0:
            @pl.when(target_core != c)
            def _():
                copy.wait_send()
        else:
            copy.wait_send()
    for copy in q_copies:
        copy.wait_recv()
    for copy in q_copies:
        copy.wait_send()


def finish_kernel(
    leaf_x, mid_x, solved, terms, leaf_out, mid_out, top_solution, outer_out, outer_v, out_sems
):
    pairs = ((leaf_x, leaf_out), (mid_x, mid_out), (solved, top_solution), (outer_v, outer_out))
    stores = [
        pltpu.make_async_copy(src, dst, out_sems.at[i]) for i, (src, dst) in enumerate(pairs)
    ]
    for store in stores[:3]:
        store.start()
    total = terms[0]
    for d in range(1, terms.shape[0]):
        total += terms[d]
    outer_v[...] = total
    stores[3].start()
    for store in stores:
        store.wait()


def on_device(
    nz, nx, ny,
    rhs_leaf, rhs_mid, rhs_top, inv_leaf, inv_mid, inv_top,
    off_leaf_mid, off_leaf_top, off_leaf_out, off_mid_top, off_mid_out, off_top_out,
    parent_leaf, parent_mid, width_leaf, width_mid, width_top, pattern_leaf, pattern_mid,
):
    hbm = pl.BlockSpec(memory_space=pl.ANY)
    vmem = pl.BlockSpec(memory_space=pltpu.VMEM)
    leaves, leaf_w, num_rhs = rhs_leaf.shape[1:]
    mids, mid_w = rhs_mid.shape[1:3]
    tops, slab = rhs_top.shape[:2]
    top_w = inv_top.shape[2]
    outer = off_leaf_out.shape[2]
    rows = off_top_out.shape[1]
    half = num_rhs // LANES
    per_y = tops // ny
    assert per_y * half == nx and slab * 2 * nx == top_w and rows * 2 * nx == outer
    half_rows = top_w // 2
    chunks = CHUNKS
    part = half_rows // chunks // 2
    wide = num_rhs // nz
    chunk = wide // ny
    group = nz // half * chunk

    def vm(*shape, dtype=BF16):
        return pltpu.VMEM(shape, dtype)

    sems = pltpu.SemaphoreType.DMA
    results = pl.pallas_call(
        functools.partial(window_kernel, nz, nx, ny),
        out_shape=(
            pltpu.VMEM(rhs_leaf.shape, BF16),
            pltpu.VMEM(rhs_mid.shape, BF16),
            pltpu.VMEM((per_y, slab, num_rhs), BF16),
            pltpu.VMEM((2 * nz, chunk, rows), F32),
        ),
        in_specs=[hbm] * 19,
        out_specs=(vmem,) * 4,
        scratch_shapes=[
            pltpu.SMEM((1, leaves), jnp.int32), pltpu.SMEM((1, mids), jnp.int32),
            pltpu.SMEM((1, leaves), jnp.int32), pltpu.SMEM((1, mids), jnp.int32),
            pltpu.SMEM((tops,), jnp.int32), pltpu.SMEM((2, leaves), jnp.int32),
            pltpu.SMEM((1, mids), jnp.int32),
            vm(leaves, leaf_w, num_rhs), vm(leaves, leaf_w, leaf_w), vm(leaves, mid_w, leaf_w),
            vm(mids, mid_w, num_rhs), vm(mids, mid_w, mid_w),
            vm(leaves, top_w, leaf_w), vm(mids, top_w, mid_w),
            vm(leaves, outer, leaf_w), vm(mids, outer, mid_w),
            vm(leaves * leaf_w + mids * mid_w, num_rhs),
            vm(mids, mid_w + 2 * leaf_w, num_rhs),
            vm(chunks, 2, mids, 2 * part, num_rhs), vm(chunks, mids, 2 * part, num_rhs),
            vm(mids, max(tops, 8), LANES, dtype=F32), vm(mids, max(tops, 8), LANES, dtype=F32),
            vm(chunks, 2, ny, nx, part, LANES),
            vm(chunks, nx - 1, ny, part, LANES), vm(chunks, ny - 1, nx, part, LANES),
            vm(chunks, ny, part, LANES), vm(chunks, nx, part, LANES),
            vm(chunks, ny - 1, part, LANES), vm(chunks, nx - 1, part, LANES),
            vm(2, chunks, 2 * part, LANES), vm(nx, slab, top_w), vm(nx, slab, LANES),
            vm(nx, slab, LANES), vm(nx, slab, LANES),
            vm(ny, group, half_rows), vm(ny, nx, group, half_rows),
            vm(tops, 2, rows, half_rows),
            vm(2, nx, nz, wide, rows), vm(nx, nz, wide, rows), vm(nx, nz, wide, rows),
            vm(nz - 1, nx, wide, rows), vm(nx, wide, rows), vm(nx - 1, wide, rows),
            vm(ny, chunk, rows, dtype=F32), vm(ny - 1, chunk, rows, dtype=F32),
            vm(2, nz, chunk, rows, dtype=F32),
            sems((7,)), sems((10,)),
            sems((3 + 2 * chunks,)), sems((3 + 2 * chunks,)),
            sems((2, nx)), sems((2, nx)),
            sems((chunks, nx - 1)), sems((chunks, nx - 1)),
            sems((chunks, ny - 1)), sems((chunks, ny - 1)),
            sems((chunks, ny - 1)), sems((chunks, ny - 1)),
            sems((chunks, nx - 1)), sems((chunks, nx - 1)),
            sems((nx,)), sems((nx,)), sems((nx * ny - 1,)), sems((nx * ny - 1,)),
            sems((nz - 1,)), sems((nz - 1,)), sems((nx - 1,)), sems((nx - 1,)),
            sems((ny - 1,)), sems((ny - 1,)), sems((2 * nz - 1,)), sems((2 * nz - 1,)),
        ],
        compiler_params=pltpu.CompilerParams(
            collective_id=0, has_side_effects=True, vmem_limit_bytes=60 << 20
        ),
        name="window",
    )(
        parent_leaf.reshape(1, leaves), parent_mid.reshape(1, mids), width_leaf, width_mid,
        width_top, jnp.transpose(pattern_leaf[0], (1, 0)), pattern_mid,
        rhs_leaf, rhs_mid, rhs_top, inv_leaf, inv_mid, inv_top,
        off_leaf_mid, off_leaf_top, off_leaf_out, off_mid_top, off_mid_out, off_top_out,
    )
    shapes = [jax.ShapeDtypeStruct(a.shape, a.dtype) for a in results[:3]]
    shapes.append(jax.ShapeDtypeStruct((chunk, rows), F32))
    leaf_x, mid_x, top_solution, outer_part = pl.pallas_call(
        finish_kernel,
        out_shape=tuple(shapes),
        in_specs=[vmem] * 4,
        out_specs=(hbm,) * 4,
        scratch_shapes=[vm(chunk, rows, dtype=F32), sems((4,))],
        compiler_params=pltpu.CompilerParams(vmem_limit_bytes=60 << 20),
        name="finish",
    )(*[pltpu.with_memory_space_constraint(a, pltpu.VMEM) for a in results])
    return leaf_x, mid_x, top_solution, outer_part.T


def solution(mesh):
    sizes = dict(mesh.shape)
    deep = P("gz", ("pr", "pc"), None, None)
    flat = P("pr", "pc", None)
    return jax.shard_map(
        functools.partial(on_device, sizes["pr"], sizes["pc"] // 2, sizes["gz"]),
        mesh=mesh,
        in_specs=(
            deep, deep, flat, deep, deep, flat,
            deep, deep, deep, deep, deep, flat,
            P("gz", ("pr", "pc"), None),
            P("gz", ("pr", "pc"), None),
            P("gz", ("pr", "pc")),
            P("gz", ("pr", "pc")),
            P("pr"),
            P("gz", ("pr", "pc"), None),
            P("gz", ("pr", "pc")),
        ),
        out_specs=(deep, deep, P(("pr", "gz"), "pc", None), P("pc", ("pr", "gz"))),
        check_vma=False,
    )
```

```python
import functools

import jax
import jax.numpy as jnp
from jax import lax
from jax.experimental import pallas as pl
from jax.experimental.pallas import tpu as pltpu
from jax.sharding import PartitionSpec as P

MESH_IDS = pl.DeviceIdType.MESH
F32 = jnp.float32
BF16 = jnp.bfloat16
LANES = 128
CHUNKS = 2


def dot(a, b):
    return jnp.dot(a, b, preferred_element_type=F32)


def live_rows(values, first_row, width):
    row_ids = first_row + lax.broadcasted_iota(jnp.int32, values.shape, 0)
    return jnp.where(row_ids < width, values, 0.0)


def flagged(values, flag):
    return jnp.where(flag != 0, values, jnp.zeros_like(values))


def dot_nt(a, b):
    return lax.dot_general(a, b, (((1,), (1,)), ((), ())), preferred_element_type=F32)


def window_kernel(
    nz, nx, ny,
    parent_leaf_in, parent_mid_in, width_leaf_in, width_mid_in, width_top_in,
    pattern_leaf_in, pattern_mid_in,
    rhs_leaf, rhs_mid, rhs_top, inv_leaf, inv_mid, inv_top,
    off_leaf_mid, off_leaf_top, off_leaf_out, off_mid_top, off_mid_out, off_top_out,
    leaf_out, mid_out, top_solution, terms_out,
    parent_leaf, parent_mid, width_leaf, width_mid, width_top, pattern_leaf, pattern_mid,
    rl, il, lm, rm, im, lt, mt, ol, om, xo, xu, up_own, up_rx, mask, mask_rx,
    t_sum, a_rx, b_rx, a_sum, b_sum, a_rx2, b_rx2, top_in, inv, rhs,
    unit, sol_rx, turned, gathered, wt,
    o_t, o_rx, o_s, o_rz, o_z, o_rx2, o_x, o_ry, q,
    vector_sems, load_sems, core_s, core_r, pre_s, pre_r, a_s, a_r, b_s, b_r, a2_s, a2_r, b2_s, b2_r,
    sol_s, sol_r, g_s, g_r, oz_s, oz_r, ox_s, ox_r, oy_s, oy_r, q_s, q_r,
):
    z = lax.axis_index("pr")
    pc = lax.axis_index("pc")
    y = lax.axis_index("gz")
    x = pc // 2
    c = pc % 2
    other = 1 - c
    sibling = 2 * x + other
    xl, xm = leaf_out.at[0], mid_out.at[0]
    leaves, mids = xl.shape[0], xm.shape[0]
    tops = rhs_top.shape[0]
    per_y = tops // ny
    half = xl.shape[2] // LANES
    slab = rhs_top.shape[1]
    chunks = t_sum.shape[0]
    part = t_sum.shape[4]
    block_rows = 2 * part
    half_rows = chunks * block_rows
    chunk = q.shape[2]
    rows = terms_out.shape[2]
    wide = o_t.shape[3]
    group = gathered.shape[2]
    num_rhs = xl.shape[2]

    def remote(src, dst, send, recv, device):
        return pltpu.make_async_remote_copy(
            src_ref=src, dst_ref=dst, send_sem=send, recv_sem=recv,
            device_id=device, device_id_type=MESH_IDS,
        )

    vectors = [
        pltpu.make_async_copy(src, dst, vector_sems.at[i]) for i, (src, dst) in enumerate((
            (width_leaf_in, width_leaf), (parent_leaf_in, parent_leaf), (parent_mid_in, parent_mid),
            (width_mid_in, width_mid), (pattern_leaf_in, pattern_leaf),
            (pattern_mid_in, pattern_mid), (width_top_in, width_top),
        ))
    ]
    load_pairs = [
        (inv_leaf.at[0], il), (rhs_leaf.at[0], rl), (off_leaf_mid.at[0], lm),
        (inv_mid.at[0], im), (rhs_mid.at[0], rm), (off_mid_top.at[0], mt), (off_leaf_top.at[0], lt),
        (off_leaf_out.at[0], ol), (off_mid_out.at[0], om),
        (off_top_out.at[:, :, pl.ds(pl.multiple_of(c * half_rows, half_rows), half_rows)], wt.at[:, c]),
    ]
    loads = [
        pltpu.make_async_copy(src, dst, load_sems.at[i]) for i, (src, dst) in enumerate(load_pairs)
    ]
    for load in loads[:2] + vectors[:4] + loads[2:5]:
        load.start()

    barrier = pltpu.get_barrier_semaphore()
    partners = []
    for d in sorted(range(1, nz), key=lambda d: -min(d, nz - d)):
        for core in range(2):
            partners.append((lax.rem(z + d, nz), 2 * x + core, y))
    steps = [(dx, dy) for dy in range(ny) for dx in range(nx) if dx or dy]
    for dx, dy in sorted(steps, key=lambda d: -min(d[0], nx - d[0]) - min(d[1], ny - d[1])):
        partners.append((z, 2 * lax.rem(x + dx, nx) + c, lax.rem(y + dy, ny)))
    for dx in range(nx):
        partners.append((z, 2 * lax.rem(x + dx, nx) + other, y))
    for partner in partners:
        pl.semaphore_signal(barrier, inc=1, device_id=partner, device_id_type=MESH_IDS)
    for load in loads[5:7] + vectors[4:]:
        load.start()
    for vector in vectors:
        vector.wait()

    parents = [lax.rem(parent_leaf[0, k], mids) for k in range(leaves)]
    first, last = [], []
    for j in range(mids):
        low = jnp.int32(0)
        high = jnp.int32(0)
        for k in range(leaves):
            high = jnp.where(parents[k] == j, k, high)
            back = leaves - 1 - k
            low = jnp.where(parents[back] == j, back, low)
        first.append(low)
        last.append(high)
    for j in range(mids):
        ids = lax.broadcasted_iota(jnp.int32, mask.shape[1:], 0)
        mask[j] = jnp.where(ids == lax.rem(parent_mid[0, j], tops), 1.0, 0.0)

    loads[0].wait()
    loads[1].wait()
    for k in range(leaves):
        xl[k] = live_rows(dot(il[k], rl[k]), 0, width_leaf[0, k]).astype(BF16)

    for load in loads[2:5]:
        load.wait()
    for j in range(mids):
        total = dot(
            jnp.concatenate([lm[first[j]], lm[last[j]]], axis=1),
            jnp.concatenate([xl[first[j]], xl[last[j]]], axis=0),
        )
        mid_input = (rm[j].astype(F32) - total).astype(BF16)
        xm[j] = live_rows(dot(im[j], mid_input), 0, width_mid[0, j]).astype(BF16)
    for load in loads[7:]:
        load.start()

    loads[5].wait()
    loads[6].wait()
    for j in range(mids):
        low, high = first[j], last[j]
        xu[j] = jnp.concatenate([
            xm[j], flagged(xl[low], pattern_leaf[0, low]), flagged(xl[high], pattern_leaf[0, high])
        ], axis=0)
    up_copies = []
    for q_ in range(chunks):
        for j in range(mids):
            low, high = first[j], last[j]
            spans = [
                pl.ds(core * half_rows + q_ * block_rows, block_rows) for core in range(2)
            ]
            update = dot(
                jnp.concatenate([
                    jnp.concatenate([mt[j, span, :], lt[low, span, :], lt[high, span, :]], axis=1)
                    for span in spans
                ], axis=0),
                xu[j],
            )
            for core in range(2):
                up_own[q_, core, j] = update[core * block_rows:(core + 1) * block_rows].astype(BF16)
        if q_ == 0:
            pl.semaphore_wait(barrier, len(partners))
            mask_copy = remote(mask, mask_rx, core_s.at[0], core_r.at[0], (z, sibling, y))
            mask_copy.start()
        up_copies.append(remote(
            up_own.at[q_, other], up_rx.at[q_], core_s.at[1 + q_], core_r.at[1 + q_], (z, sibling, y)
        ))
        up_copies[-1].start()
    last_sem = 1 + chunks
    w_copy = remote(
        off_top_out.at[:, :, pl.ds(pl.multiple_of(other * half_rows, half_rows), half_rows)],
        wt.at[:, c], core_s.at[last_sem], core_r.at[last_sem], (z, sibling, y),
    )

    mask_copy.wait_recv()
    step = 16
    far_x = sorted(range(1, nx), key=lambda d: -min(d, nx - d))
    far_y = sorted(range(1, ny), key=lambda d: -min(d, ny - d))
    a_copies, b_copies = [], []
    for q_ in range(chunks):
        up_copies[q_].wait_recv()
        for p in range(2):
            def pair_sum(i, carry):
                at = pl.multiple_of(i * step, step)
                span = pl.ds(pl.multiple_of(p * part + at, step), step)
                blocks = [up_own[q_, c, j, span, :].astype(F32) for j in range(mids)]
                blocks += [up_rx[q_, j, span, :].astype(F32) for j in range(mids)]
                for s in range(tops):
                    for h in range(half):
                        total = jnp.zeros((step, LANES), F32)
                        for j in range(2 * mids):
                            table = mask if j < mids else mask_rx
                            weight = table[j % mids, s:s + 1, :]
                            total += weight * blocks[j][:, h * LANES:(h + 1) * LANES]
                        t_sum[q_, p, s // per_y, (s % per_y) * half + h, pl.ds(at, step), :] = (
                            total.astype(BF16)
                        )
                return carry

            lax.fori_loop(0, part // step, pair_sum, 0)
            if p == 0:
                a_copies.append([])
                for d in far_x:
                    tx = lax.rem(x + d, nx)
                    a_copies[q_].append(remote(
                        t_sum.at[q_, 0, :, tx], a_rx.at[q_, d - 1],
                        a_s.at[q_, d - 1], a_r.at[q_, d - 1], (z, 2 * tx + c, y),
                    ))
                    a_copies[q_][-1].start()
            else:
                b_copies.append([])
                for d in far_y:
                    ty = lax.rem(y + d, ny)
                    b_copies[q_].append(remote(
                        t_sum.at[q_, 1, ty], b_rx.at[q_, d - 1],
                        b_s.at[q_, d - 1], b_r.at[q_, d - 1], (z, pc, ty),
                    ))
                    b_copies[q_][-1].start()
    slot = lax.rem(pc, nx)
    target_core = pc // nx
    pre_copies = []
    for d in range(nx):
        tx = lax.rem(x + d, nx)
        s = y * per_y + tx // half
        column = pl.multiple_of(lax.rem(tx, half) * LANES, LANES)
        pairs = (
            (inv_top.at[s], inv.at[slot]),
            (rhs_top.at[s, :, pl.ds(column, LANES)], rhs.at[slot]),
        )
        for i, (src, dst) in enumerate(pairs):
            copy = remote(
                src, dst, pre_s.at[i, d], pre_r.at[i, slot], (z, 2 * tx + target_core, y)
            )
            pre_copies.append((d, copy))
            if d == 0:
                @pl.when(target_core == c)
                def _():
                    pltpu.make_async_copy(src, dst, pre_r.at[i, slot]).start()

                @pl.when(target_core != c)
                def _():
                    copy.start()
            else:
                copy.start()

    w_copy.start()

    leaf_w, mid_w = xl.shape[1], xm.shape[1]
    for k in range(leaves):
        xo[k * leaf_w:(k + 1) * leaf_w] = flagged(xl[k], pattern_leaf[1, k])
    base = leaves * leaf_w
    for j in range(mids):
        xo[base + j * mid_w:base + (j + 1) * mid_w] = flagged(xm[j], pattern_mid[0, j])
    loads[7].wait()
    loads[8].wait()

    def outer_rows(i, carry):
        block = pl.ds(pl.multiple_of(i * 2 * rows, 2 * rows), 2 * rows)
        total = dot(
            jnp.concatenate(
                [ol[k, block, :] for k in range(leaves)] + [om[j, block, :] for j in range(mids)],
                axis=1,
            ),
            xo[...],
        )
        for core in range(2):
            across = total[core * rows:(core + 1) * rows].T
            o_t[core, i] = across.reshape(nz, wide, rows).astype(BF16)
        return carry

    lax.fori_loop(0, nx, outer_rows, 0)
    o_core = remote(
        o_t.at[other], o_rx, core_s.at[last_sem + 1], core_r.at[last_sem + 1], (z, sibling, y)
    )
    o_core.start()

    a2_copies, b2_copies = [], []
    for q_ in range(chunks):
        for copy in a_copies[q_]:
            copy.wait_recv()
        for i in range(ny):
            total = t_sum[q_, 0, i, x].astype(F32)
            for d in range(nx - 1):
                total += a_rx[q_, d, i].astype(F32)
            a_sum[q_, i] = total.astype(BF16)
        a2_copies.append([])
        for d in far_y:
            ty = lax.rem(y + d, ny)
            a2_copies[q_].append(remote(
                a_sum.at[q_, ty], a_rx2.at[q_, d - 1],
                a2_s.at[q_, d - 1], a2_r.at[q_, d - 1], (z, pc, ty),
            ))
            a2_copies[q_][-1].start()
        for copy in b_copies[q_]:
            copy.wait_recv()
        for i in range(nx):
            total = t_sum[q_, 1, y, i].astype(F32)
            for d in range(ny - 1):
                total += b_rx[q_, d, i].astype(F32)
            b_sum[q_, i] = total.astype(BF16)
        b2_copies.append([])
        for d in far_x:
            tx = lax.rem(x + d, nx)
            b2_copies[q_].append(remote(
                b_sum.at[q_, tx], b_rx2.at[q_, d - 1],
                b2_s.at[q_, d - 1], b2_r.at[q_, d - 1], (z, 2 * tx + c, y),
            ))
            b2_copies[q_][-1].start()
    o_core.wait_recv()
    oz_copies = []

    def outer_pair(i, carry):
        o_s[i] = (o_t[c, i].astype(F32) + o_rx[i].astype(F32)).astype(BF16)
        return carry

    lax.fori_loop(0, nx, outer_pair, 0)
    for d in range(1, nz):
        tz = lax.rem(z + d, nz)
        oz_copies.append(remote(
            o_s.at[:, tz], o_rz.at[d - 1], oz_s.at[d - 1], oz_r.at[d - 1], (tz, pc, y),
        ))
        oz_copies[-1].start()

    for i in range(nx):
        pre = [
            remote(inv_top.at[0], inv.at[i], pre_s.at[0, 0], pre_r.at[0, i], (z, sibling, y)),
            remote(rhs_top.at[0, :, pl.ds(0, LANES)], rhs.at[i], pre_s.at[1, 0], pre_r.at[1, i],
                   (z, sibling, y)),
        ]
        for copy in pre:
            copy.wait_recv()
    right = rhs[...].reshape(chunks, 2, part, LANES).astype(F32)
    in_copies = []
    for q_ in range(chunks):
        for copy in a2_copies[q_]:
            copy.wait_recv()
        total = a_sum[q_, y].astype(F32)
        for d in range(ny - 1):
            total += a_rx2[q_, d].astype(F32)
        top_in[c, q_, pl.ds(0, part), :] = (right[q_, 0] - total).astype(BF16)
        for copy in b2_copies[q_]:
            copy.wait_recv()
        total = b_sum[q_, x].astype(F32)
        for d in range(nx - 1):
            total += b_rx2[q_, d].astype(F32)
        top_in[c, q_, pl.ds(part, part), :] = (right[q_, 1] - total).astype(BF16)
        i = last_sem + 2 + q_
        in_copies.append(remote(
            top_in.at[c, q_], top_in.at[c, q_], core_s.at[i], core_r.at[i], (z, sibling, y)
        ))
        in_copies[-1].start()
    for copy in in_copies:
        copy.wait_recv()

    block = dot(inv[...].reshape(half_rows, inv.shape[2]), top_in[...].reshape(2 * half_rows, LANES))
    block = live_rows(block, c * half_rows, width_top[y * per_y + x // half])
    across = block.T.reshape(nz // half, ny, chunk, half_rows)
    for i in range(ny):
        turned[i] = across[:, i].reshape(group, half_rows).astype(BF16)
    unit[...] = block.reshape(nx, slab, LANES).astype(BF16)

    g_copies = []
    steps = [(dx, dy) for dy in range(ny) for dx in range(nx) if dx or dy]
    for dx, dy in sorted(steps, key=lambda d: -min(d[0], nx - d[0]) - min(d[1], ny - d[1])):
        tx = lax.rem(x + dx, nx)
        ty = lax.rem(y + dy, ny)
        i = dy * nx + dx - 1
        g_copies.append(remote(
            turned.at[ty], gathered.at[y, x], g_s.at[i], g_r.at[i], (z, 2 * tx + c, ty),
        ))
        g_copies[-1].start()
    gathered[y, x] = turned[y]

    sol_copies = []
    for d in range(nx):
        i = lax.rem(slot + d, nx)
        copy = remote(
            unit.at[i], sol_rx.at[x], sol_s.at[d], sol_r.at[x], (z, nx * c + i, y)
        )
        sol_copies.append((d, copy))
        if d == 0:
            @pl.when(target_core == c)
            def _():
                pltpu.make_async_copy(unit.at[i], sol_rx.at[x], sol_r.at[x]).start()

            @pl.when(target_core != c)
            def _():
                copy.start()
        else:
            copy.start()

    for copy in oz_copies:
        copy.wait_recv()
    ox_copies = []
    for i in range(nx):
        total = o_s[i, z].astype(F32)
        for d in range(nz - 1):
            total += o_rz[d, i].astype(F32)
        o_z[i] = total.astype(BF16)
    for d in range(1, nx):
        tx = lax.rem(x + d, nx)
        ox_copies.append(remote(
            o_z.at[tx], o_rx2.at[d - 1], ox_s.at[d - 1], ox_r.at[d - 1], (z, 2 * tx + c, y),
        ))
        ox_copies[-1].start()

    loads[9].wait()
    w_copy.wait_recv()
    for copy in g_copies:
        copy.wait_recv()

    total = jnp.zeros((half * group, 2 * rows), F32)
    for i in range(ny):
        for t in range(per_y):
            left = gathered[i, t * half:(t + 1) * half].reshape(half * group, half_rows)
            total += dot_nt(left, wt[i * per_y + t].reshape(2 * rows, half_rows))
    for core in range(2):
        q[core] = total[:, core * rows:(core + 1) * rows].reshape(nz, chunk, rows)
    q_copies = []
    steps = [(dz, dc) for dz in range(nz) for dc in range(2) if dz or dc]
    for dz, dc in sorted(steps, key=lambda d: -min(d[0], nz - d[0])):
        tz = lax.rem(z + dz, nz)
        tc = lax.rem(c + dc, 2)
        i = 2 * dz + dc - 1
        q_copies.append(remote(
            q.at[tc, tz], terms_out.at[i], q_s.at[i], q_r.at[i], (tz, 2 * x + tc, y),
        ))
        q_copies[-1].start()

    for copy in ox_copies:
        copy.wait_recv()
    total = o_z[x].astype(F32)
    for d in range(nx - 1):
        total += o_rx2[d].astype(F32)
    o_x[...] = total.reshape(ny, chunk, rows)
    oy_copies = []
    for d in range(1, ny):
        ty = lax.rem(y + d, ny)
        oy_copies.append(remote(
            o_x.at[ty], o_ry.at[d - 1], oy_s.at[d - 1], oy_r.at[d - 1], (z, pc, ty),
        ))
        oy_copies[-1].start()
    for i in range(nx):
        remote(unit.at[0], sol_rx.at[i], sol_s.at[0], sol_r.at[i], (z, sibling, y)).wait_recv()
    for t in range(per_y):
        for h in range(half):
            top_solution[t, :, h * LANES:(h + 1) * LANES] = sol_rx[t * half + h]
    for copy in oy_copies:
        copy.wait_recv()
    total = o_x[y]
    for d in range(ny - 1):
        total += o_ry[d]
    terms_out[2 * nz - 1] = total + q[c, z]

    for copy in (
        [mask_copy, w_copy, o_core] + in_copies + up_copies
        + sum(a_copies + b_copies + a2_copies + b2_copies, [])
        + g_copies + oz_copies + ox_copies + oy_copies
    ):
        copy.wait_send()
    for d, copy in pre_copies + sol_copies:
        if d == 0:
            @pl.when(target_core != c)
            def _():
                copy.wait_send()
        else:
            copy.wait_send()
    for copy in q_copies:
        copy.wait_recv()
    for copy in q_copies:
        copy.wait_send()


def finish_kernel(
    leaf_x, mid_x, solved, terms, leaf_out, mid_out, top_solution, outer_out, outer_v, out_sems
):
    pairs = ((leaf_x, leaf_out), (mid_x, mid_out), (solved, top_solution), (outer_v, outer_out))
    stores = [
        pltpu.make_async_copy(src, dst, out_sems.at[i]) for i, (src, dst) in enumerate(pairs)
    ]
    for store in stores[:3]:
        store.start()
    total = terms[0]
    for d in range(1, terms.shape[0]):
        total += terms[d]
    outer_v[...] = total
    stores[3].start()
    for store in stores:
        store.wait()


def on_device(
    nz, nx, ny,
    rhs_leaf, rhs_mid, rhs_top, inv_leaf, inv_mid, inv_top,
    off_leaf_mid, off_leaf_top, off_leaf_out, off_mid_top, off_mid_out, off_top_out,
    parent_leaf, parent_mid, width_leaf, width_mid, width_top, pattern_leaf, pattern_mid,
):
    hbm = pl.BlockSpec(memory_space=pl.ANY)
    vmem = pl.BlockSpec(memory_space=pltpu.VMEM)
    leaves, leaf_w, num_rhs = rhs_leaf.shape[1:]
    mids, mid_w = rhs_mid.shape[1:3]
    tops, slab = rhs_top.shape[:2]
    top_w = inv_top.shape[2]
    outer = off_leaf_out.shape[2]
    rows = off_top_out.shape[1]
    half = num_rhs // LANES
    per_y = tops // ny
    assert per_y * half == nx and slab * 2 * nx == top_w and rows * 2 * nx == outer
    half_rows = top_w // 2
    chunks = CHUNKS
    part = half_rows // chunks // 2
    wide = num_rhs // nz
    chunk = wide // ny
    group = nz // half * chunk

    def vm(*shape, dtype=BF16):
        return pltpu.VMEM(shape, dtype)

    sems = pltpu.SemaphoreType.DMA
    results = pl.pallas_call(
        functools.partial(window_kernel, nz, nx, ny),
        out_shape=(
            pltpu.VMEM(rhs_leaf.shape, BF16),
            pltpu.VMEM(rhs_mid.shape, BF16),
            pltpu.VMEM((per_y, slab, num_rhs), BF16),
            pltpu.VMEM((2 * nz, chunk, rows), F32),
        ),
        in_specs=[hbm] * 19,
        out_specs=(vmem,) * 4,
        scratch_shapes=[
            pltpu.SMEM((1, leaves), jnp.int32), pltpu.SMEM((1, mids), jnp.int32),
            pltpu.SMEM((1, leaves), jnp.int32), pltpu.SMEM((1, mids), jnp.int32),
            pltpu.SMEM((tops,), jnp.int32), pltpu.SMEM((2, leaves), jnp.int32),
            pltpu.SMEM((1, mids), jnp.int32),
            vm(leaves, leaf_w, num_rhs), vm(leaves, leaf_w, leaf_w), vm(leaves, mid_w, leaf_w),
            vm(mids, mid_w, num_rhs), vm(mids, mid_w, mid_w),
            vm(leaves, top_w, leaf_w), vm(mids, top_w, mid_w),
            vm(leaves, outer, leaf_w), vm(mids, outer, mid_w),
            vm(leaves * leaf_w + mids * mid_w, num_rhs),
            vm(mids, mid_w + 2 * leaf_w, num_rhs),
            vm(chunks, 2, mids, 2 * part, num_rhs), vm(chunks, mids, 2 * part, num_rhs),
            vm(mids, max(tops, 8), LANES, dtype=F32), vm(mids, max(tops, 8), LANES, dtype=F32),
            vm(chunks, 2, ny, nx, part, LANES),
            vm(chunks, nx - 1, ny, part, LANES), vm(chunks, ny - 1, nx, part, LANES),
            vm(chunks, ny, part, LANES), vm(chunks, nx, part, LANES),
            vm(chunks, ny - 1, part, LANES), vm(chunks, nx - 1, part, LANES),
            vm(2, chunks, 2 * part, LANES), vm(nx, slab, top_w), vm(nx, slab, LANES),
            vm(nx, slab, LANES), vm(nx, slab, LANES),
            vm(ny, group, half_rows), vm(ny, nx, group, half_rows),
            vm(tops, 2, rows, half_rows),
            vm(2, nx, nz, wide, rows), vm(nx, nz, wide, rows), vm(nx, nz, wide, rows),
            vm(nz - 1, nx, wide, rows), vm(nx, wide, rows), vm(nx - 1, wide, rows),
            vm(ny, chunk, rows, dtype=F32), vm(ny - 1, chunk, rows, dtype=F32),
            vm(2, nz, chunk, rows, dtype=F32),
            sems((7,)), sems((10,)),
            sems((3 + 2 * chunks,)), sems((3 + 2 * chunks,)),
            sems((2, nx)), sems((2, nx)),
            sems((chunks, nx - 1)), sems((chunks, nx - 1)),
            sems((chunks, ny - 1)), sems((chunks, ny - 1)),
            sems((chunks, ny - 1)), sems((chunks, ny - 1)),
            sems((chunks, nx - 1)), sems((chunks, nx - 1)),
            sems((nx,)), sems((nx,)), sems((nx * ny - 1,)), sems((nx * ny - 1,)),
            sems((nz - 1,)), sems((nz - 1,)), sems((nx - 1,)), sems((nx - 1,)),
            sems((ny - 1,)), sems((ny - 1,)), sems((2 * nz - 1,)), sems((2 * nz - 1,)),
        ],
        compiler_params=pltpu.CompilerParams(
            collective_id=0, has_side_effects=True, vmem_limit_bytes=60 << 20
        ),
        name="window",
    )(
        parent_leaf.reshape(1, leaves), parent_mid.reshape(1, mids), width_leaf, width_mid,
        width_top, jnp.transpose(pattern_leaf[0], (1, 0)), pattern_mid,
        rhs_leaf, rhs_mid, rhs_top, inv_leaf, inv_mid, inv_top,
        off_leaf_mid, off_leaf_top, off_leaf_out, off_mid_top, off_mid_out, off_top_out,
    )
    shapes = [jax.ShapeDtypeStruct(a.shape, a.dtype) for a in results[:3]]
    shapes.append(jax.ShapeDtypeStruct((chunk, rows), F32))
    leaf_x, mid_x, top_solution, outer_part = pl.pallas_call(
        finish_kernel,
        out_shape=tuple(shapes),
        in_specs=[vmem] * 4,
        out_specs=(hbm,) * 4,
        scratch_shapes=[vm(chunk, rows, dtype=F32), sems((4,))],
        compiler_params=pltpu.CompilerParams(vmem_limit_bytes=60 << 20),
        name="finish",
    )(*[pltpu.with_memory_space_constraint(a, pltpu.VMEM) for a in results])
    return leaf_x, mid_x, top_solution, outer_part.T


def solution(mesh):
    sizes = dict(mesh.shape)
    deep = P("gz", ("pr", "pc"), None, None)
    flat = P("pr", "pc", None)
    return jax.shard_map(
        functools.partial(on_device, sizes["pr"], sizes["pc"] // 2, sizes["gz"]),
        mesh=mesh,
        in_specs=(
            deep, deep, flat, deep, deep, flat,
            deep, deep, deep, deep, deep, flat,
            P("gz", ("pr", "pc"), None),
            P("gz", ("pr", "pc"), None),
            P("gz", ("pr", "pc")),
            P("gz", ("pr", "pc")),
            P("pr"),
            P("gz", ("pr", "pc"), None),
            P("gz", ("pr", "pc")),
        ),
        out_specs=(deep, deep, P(("pr", "gz"), "pc", None), P("pc", ("pr", "gz"))),
        check_vma=False,
    )
```
